32 devices in a mesh: ctx: 8 (over z, y), fsdp: 4 (over x, core).
Axes of the slice: x: 2, y: 2, z: 4, core: 2. Of those that a mesh axis runs over, the one named last changes fastest.
Arguments:
- inputs: bfloat16 [2048, 7168], P('ctx'), may hold values from -12 to 12
- w_qkv: bfloat16 [7168, 3, 1024], P('ctx', None, 'fsdp'), may hold values from -1 to 1, as said below
- selected: int32 [4, 4], replicated, may hold values from -1 to 3, as said below
- d_attn: bfloat16 [2048, 1024], P('ctx', 'fsdp'), may hold values from -6 to 6
Outputs:
- d_input: bfloat16 [2048, 7168], P('ctx', 'fsdp')
The draws below stay inside these ranges and needn't reach their ends.
Inputs may be any that keep to these rules, and one draw needn't show every extreme that they name: `selected`: row b lists min(b + 1, 4) different blocks of 0 to b, b among them, in the first slots; the other slots hold -1. `w_qkv`: projection weights scaled by the fan-in.
All inputs are finite; a program needn't handle non-finite values.
Results may differ from the reference program's by a relative error of at most 0.023.
Values may be sent and summed in bfloat16 or wider, within the bound.
No kernel may reach another device: no remote copies, remote signals or barrier semaphores. Data moves between devices by JAX's collectives and lax.ppermute only.
A program may use at most 128 MiB of HBM per device.

```python
import jax
import jax.numpy as jnp
from jax import lax

D = 7168
HD = 128
H_DEV = 2
BLOCK = 512
TOP = 4
TOK_DEV = 256
HEADS = 8
SEQ = 2048
NBLK = 4
N_CTX = 8
N_FSDP = 4


def draw_inputs(key, part):
    base = jnp.clip(jax.random.normal(key, (SEQ, D), jnp.float32), -6.0, 6.0)
    return base.astype(jnp.bfloat16)


def draw_w_qkv(key, part):
    base = jnp.clip(jax.random.normal(key, (D, 3, HEADS * HD), jnp.float32), -6.0, 6.0) * D ** (-0.5)
    return base.astype(jnp.bfloat16)


def draw_selected(key, part):
    first_key = jax.random.fold_in(key, 21)
    second_key = jax.random.fold_in(key, 22)
    noise = jax.random.randint(first_key, (NBLK, NBLK), 0, 4096)
    popular = jax.random.randint(second_key, (NBLK,), 0, 4)
    row_ids = jnp.arange(NBLK, dtype=jnp.int32)[:, None]
    col_ids = jnp.arange(NBLK, dtype=jnp.int32)[None, :]
    score = (noise + popular[None, :] * 4096) * NBLK + col_ids
    score = jnp.where(col_ids == row_ids, -1, score)
    score = jnp.where(col_ids > row_ids, 1 << 30, score)
    order = jnp.argsort(score, axis=1, stable=True)[:, :TOP].astype(jnp.int32)
    slot_ids = jnp.arange(TOP, dtype=jnp.int32)[None, :]
    return jnp.where(slot_ids <= row_ids, order, -1).astype(jnp.int32)


def block_levels(stream_key, shape, cuts, least, high):
    loudness = 1.0
    for dim, shards_of in cuts:
        steps = jax.random.uniform(jax.random.fold_in(jax.random.fold_in(stream_key, 6), dim), (shards_of,), jnp.float32, least / len(cuts), high / len(cuts))
        loudness = loudness * jnp.repeat(jnp.exp(steps), shape[dim] // shards_of).reshape((-1,) + (1,) * (len(shape) - 1 - dim))
    return loudness


def bell_draw(rng, extent, spread, most, split=(), kind=jnp.bfloat16):
    array = spread * jax.random.normal(rng, extent, jnp.float32)
    if split:
        array = array * block_levels(rng, extent, split, -0.22, 0.18)
    return jnp.clip(array, -most, most).astype(kind)


def setup_inputs(seed: int = 0) -> dict:
    seeds = jax.random.split(jax.random.key(seed), 5)
    inputs = draw_inputs(jax.random.fold_in(seeds[4], 71), 0)
    w_qkv = draw_w_qkv(jax.random.fold_in(seeds[4], 71), 0)
    selected = draw_selected(jax.random.fold_in(seeds[4], 71), 0)
    d_attn = bell_draw(seeds[3], (SEQ, HEADS * HD), 1.0, 6.0, ((0, 8), (1, 4)))
    return dict(inputs=inputs, w_qkv=w_qkv, selected=selected, d_attn=d_attn)


def reference(inputs, w_qkv, selected, d_attn):
    scaling = HD ** -0.5
    col_total = HEADS * HD
    flat_w = w_qkv.reshape(D, 3 * col_total)
    projected = jnp.dot(inputs, flat_w, preferred_element_type=jnp.float32).astype(jnp.bfloat16)
    projected = projected.reshape(SEQ, 3, HEADS, HD)
    block_ids = jnp.arange(NBLK, dtype=jnp.int32)
    chosen = jnp.any(selected[:, :, None] == block_ids[None, None, :], axis=1)
    position = jnp.arange(SEQ, dtype=jnp.int32)
    owner = position // BLOCK
    allowed = chosen[owner][:, owner] & (position[:, None] >= position[None, :])
    grad_out = d_attn.reshape(SEQ, HEADS, HD)
    stacked = (projected[:, 0].transpose(1, 0, 2), projected[:, 1].transpose(1, 0, 2),
               projected[:, 2].transpose(1, 0, 2), grad_out.transpose(1, 0, 2))

    def one_head(item):
        query, keys, values, grad_head = item
        scores = jnp.dot(query, keys.T, preferred_element_type=jnp.float32) * scaling
        masked = jnp.where(allowed, scores, -jnp.inf)
        highest = jnp.max(masked, axis=1, keepdims=True)
        expo = jnp.exp(masked - highest)
        probs = expo / jnp.sum(expo, axis=1, keepdims=True)
        probs_low = probs.astype(jnp.bfloat16)
        attended = jnp.dot(probs_low, values, preferred_element_type=jnp.float32).astype(jnp.bfloat16)
        delta = jnp.sum(grad_head.astype(jnp.float32) * attended.astype(jnp.float32), axis=1, keepdims=True)
        dprobs = jnp.dot(grad_head, values.T, preferred_element_type=jnp.float32)
        dscores = (probs * (dprobs - delta)).astype(jnp.bfloat16)
        dquery = (jnp.dot(dscores, keys, preferred_element_type=jnp.float32) * scaling).astype(jnp.bfloat16)
        runs = (dscores.reshape(N_CTX, TOK_DEV, SEQ), query.reshape(N_CTX, TOK_DEV, HD),
                probs_low.reshape(N_CTX, TOK_DEV, SEQ), grad_head.reshape(N_CTX, TOK_DEV, HD))

        def add_run(carry, run):
            ds_run, query_run, probs_run, grad_run = run
            key_part = (jnp.dot(ds_run.T, query_run, preferred_element_type=jnp.float32) * scaling).astype(jnp.bfloat16)
            value_part = jnp.dot(probs_run.T, grad_run, preferred_element_type=jnp.float32).astype(jnp.bfloat16)
            key_part, value_part = lax.optimization_barrier((key_part, value_part))
            return (carry[0] + key_part.astype(jnp.float32), carry[1] + value_part.astype(jnp.float32)), None

        zeros_run = jnp.zeros((SEQ, HD), jnp.float32)
        (dkeys, dvalues), _ = lax.scan(add_run, (zeros_run, zeros_run), runs)
        return dquery, dkeys.astype(jnp.bfloat16), dvalues.astype(jnp.bfloat16)

    dquery, dkeys, dvalues = lax.map(one_head, stacked)
    grads = jnp.stack([dquery, dkeys, dvalues], axis=0).transpose(2, 0, 1, 3)
    group_cols = H_DEV * HD
    grad_groups = grads.reshape(SEQ, 3, N_FSDP, group_cols).transpose(2, 0, 1, 3).reshape(N_FSDP, SEQ, 3 * group_cols)
    weight_groups = w_qkv.reshape(D, 3, N_FSDP, group_cols).transpose(2, 0, 1, 3).reshape(N_FSDP, D, 3 * group_cols)

    def add_group(carry, pair):
        part = lax.dot_general(pair[0], pair[1], (((1,), (1,)), ((), ())),
                               preferred_element_type=jnp.float32).astype(jnp.bfloat16)
        part = lax.optimization_barrier(part)
        return carry + part.astype(jnp.float32), None

    total, _ = lax.scan(add_group, jnp.zeros((SEQ, D), jnp.float32), (grad_groups, weight_groups))
    return total.astype(jnp.bfloat16)
```

```python
import functools

import jax
import jax.numpy as jnp
from jax import lax
from jax.experimental import pallas as pl
from jax.experimental.pallas import tpu as pltpu
from jax.sharding import PartitionSpec as P

HD = 128
BLOCK = 512
FAR = 1 << 20
PAIR = 2
F32 = jnp.float32
BF16 = jnp.bfloat16
VMEM_LIMIT = 48 * 1024 * 1024


def swap(array, axis, size, distance):
    return lax.ppermute(array, axis, [(i, i ^ distance) for i in range(size)])


def dot_nt(a, b):
    return lax.dot_general(a, b, (((1,), (1,)), ((), ())), preferred_element_type=F32)


def dot_nn(a, b):
    return lax.dot_general(a, b, (((1,), (0,)), ((), ())), preferred_element_type=F32)


def masked_scores(products, gap, limits, run):
    scaled = products * (HD ** -0.5)
    parts = [
        jnp.where(gap <= limit, scaled[:, i * run : (i + 1) * run], -jnp.inf)
        for i, limit in enumerate(limits)
    ]
    return jnp.concatenate(parts, axis=1)


def query_kernel(sets, run, limit_ref, q_ref, grad_ref, *refs):
    kv_refs, (dq_ref, stat_ref) = refs[:sets], refs[sets:]
    gap = lax.broadcasted_iota(jnp.int32, (run, run), 1) - lax.broadcasted_iota(
        jnp.int32, (run, run), 0
    )
    lane = lax.broadcasted_iota(jnp.int32, (run, HD), 1)
    for half in range(2):
        rows = pl.ds(half * run, run)
        q, grad = q_ref[rows, :], grad_ref[rows, :]
        scores = [
            masked_scores(
                dot_nt(q, kv_refs[j][:, :HD]),
                gap,
                [limit_ref[half, 2 * j], limit_ref[half, 2 * j + 1]],
                run,
            )
            for j in range(sets)
        ]
        highest = functools.reduce(
            jnp.maximum, [jnp.max(s, axis=1, keepdims=True) for s in scores]
        )
        expo = [jnp.exp(s - highest) for s in scores]
        total = sum(jnp.sum(e, axis=1, keepdims=True) for e in expo)
        inverse = 1.0 / total
        probs = [e * inverse for e in expo]
        attended = sum(
            dot_nn(p.astype(BF16), kv_refs[j][:, HD:]) for j, p in enumerate(probs)
        ).astype(BF16)
        delta = jnp.sum(
            grad.astype(F32) * attended.astype(F32), axis=1, keepdims=True
        )
        dq = jnp.zeros((run, HD), F32)
        for j, p in enumerate(probs):
            dprobs = dot_nt(grad, kv_refs[j][:, HD:])
            dscores = (p * (dprobs - delta)).astype(BF16)
            dq += dot_nn(dscores, kv_refs[j][:, :HD])
        dq_ref[rows, :] = (dq * (HD ** -0.5)).astype(BF16)
        stats = jnp.where(
            lane == 0, highest, jnp.where(lane == 1, inverse, delta)
        )
        stat_ref[:, rows] = jnp.transpose(stats)[:8]


def key_kernel(sets, run, limit_ref, kv_ref, *refs):
    q_refs, grad_refs, stat_refs = refs[:sets], refs[sets : 2 * sets], refs[2 * sets : 3 * sets]
    out_ref = refs[3 * sets]
    gap = lax.broadcasted_iota(jnp.int32, (run, run), 0) - lax.broadcasted_iota(
        jnp.int32, (run, run), 1
    )
    for half in range(2):
        rows = pl.ds(half * run, run)
        keys, values = kv_ref[rows, :HD], kv_ref[rows, HD:]
        dk = jnp.zeros((run, HD), F32)
        dv = jnp.zeros((run, HD), F32)
        for j in range(sets):
            q, grad, stat = q_refs[j][...], grad_refs[j][...], stat_refs[j]
            scores = masked_scores(
                dot_nt(keys, q),
                gap,
                [limit_ref[half, 2 * j], limit_ref[half, 2 * j + 1]],
                run,
            )
            probs = jnp.exp(scores - stat[0:1, :]) * stat[1:2, :]
            dprobs = dot_nt(values, grad)
            dscores = (probs * (dprobs - stat[2:3, :])).astype(BF16)
            dk += dot_nn(dscores, q)
            dv += dot_nn(probs.astype(BF16), grad)
        out_ref[rows, :HD] = (dk * (HD ** -0.5)).astype(BF16)
        out_ref[rows, HD:] = dv.astype(BF16)


def local_call(kernel, out_shape, n_vmem, flops):
    return pl.pallas_call(
        kernel,
        out_shape=out_shape,
        in_specs=[pl.BlockSpec(memory_space=pltpu.SMEM)]
        + [pl.BlockSpec(memory_space=pltpu.VMEM)] * n_vmem,
        out_specs=jax.tree.map(lambda _: pl.BlockSpec(memory_space=pltpu.VMEM), out_shape),
        compiler_params=pltpu.CompilerParams(vmem_limit_bytes=VMEM_LIMIT),
        cost_estimate=pl.CostEstimate(flops=flops, bytes_accessed=4 << 20, transcendentals=1 << 20),
    )


def shards(n_ctx, n_f, inputs, w_qkv, selected, d_attn):
    run, width = inputs.shape
    depth = w_qkv.shape[0]
    per_f = width // n_f
    c = lax.axis_index("ctx")
    f = lax.axis_index("fsdp")
    mine = (c // PAIR) % 2
    over_ctx = functools.partial(swap, axis="ctx", size=n_ctx)
    over_f = functools.partial(swap, axis="fsdp", size=n_f)
    even = [d for d in range(n_ctx) if d % 2 == 0]
    group = [d for d in range(n_ctx) if not d & PAIR]
    sets = len(group)

    def head_of(array, which):
        return lax.dynamic_slice_in_dim(array, which * HD, HD, axis=array.ndim - 1)

    own_w = head_of(w_qkv, mine)
    other_w = head_of(w_qkv, 1 - mine)
    kv_of = lambda w: jnp.concatenate([w[:, 1], w[:, 2]], axis=1)
    q_of = lambda w: w[:, 0]

    def gather_pieces(own, other):
        pieces = {0: own}
        for d in even[1:]:
            pieces[d] = over_ctx(other if d & PAIR else own, distance=d)
        for d in even:
            pieces[d ^ 1] = over_ctx(pieces[d], distance=1)
        return pieces

    part = lax.dynamic_slice_in_dim(inputs, f * per_f, per_f, axis=1)
    parts = {0: over_ctx(part, distance=PAIR)}
    bit = n_f // 2
    while bit:
        for e in list(parts):
            parts[e ^ bit] = over_f(parts[e], distance=bit)
        bit //= 2
    both = jnp.concatenate([inputs, jnp.zeros_like(inputs)], axis=0)
    for e, value in parts.items():
        both = lax.dynamic_update_slice(both, value, (run, (f ^ e) * per_f))

    kv_pieces = gather_pieces(kv_of(own_w), kv_of(other_w))
    q_pieces = gather_pieces(q_of(own_w), q_of(other_w))

    def project(pieces):
        total = None
        for d, w in pieces.items():
            rows = lax.dynamic_slice_in_dim(both, (c ^ d) * depth, depth, axis=1)
            term = dot_nn(rows, w)
            total = term if total is None else total + term
        return total.astype(BF16)

    own_grad = head_of(d_attn, mine)
    grad = jnp.concatenate(
        [own_grad, over_ctx(head_of(d_attn, 1 - mine), distance=PAIR)], axis=0
    )
    grads = [grad] + [over_ctx(grad, distance=d) for d in group[1:]]

    kv = project(kv_pieces)
    kvs = [kv] + [over_ctx(kv, distance=d) for d in group[1:]]
    q = project(q_pieces)
    qs = [q] + [over_ctx(q, distance=d) for d in group[1:]]

    order = jnp.stack([c ^ d ^ p for d in group for p in (0, PAIR)])
    blocks = order * run // BLOCK
    here = order[:2]

    def limits(query_runs, key_runs, query_blocks, key_blocks):
        chosen = jnp.any(
            selected[query_blocks][:, :, None] == key_blocks[None, None, :], axis=1
        )
        ahead = query_runs[:, None] - key_runs[None, :]
        bound = jnp.where(ahead > 0, FAR, jnp.where(ahead == 0, 0, -FAR))
        return jnp.where(chosen, bound, -FAR).astype(jnp.int32)

    query_limits = limits(here, order, blocks[:2], blocks)
    key_limits = limits(order, here, blocks, blocks[:2]).T

    dq, stat = local_call(
        functools.partial(query_kernel, sets, run),
        (
            jax.ShapeDtypeStruct((2 * run, HD), BF16),
            jax.ShapeDtypeStruct((8, 2 * run), F32),
        ),
        2 + sets,
        2 * 2 * run * sets * 2 * run * HD * 5,
    )(query_limits, q, grad, *kvs)
    stats = [stat] + [over_ctx(stat, distance=d) for d in group[1:]]
    dkv = local_call(
        functools.partial(key_kernel, sets, run),
        jax.ShapeDtypeStruct((2 * run, 2 * HD), BF16),
        1 + 3 * sets,
        2 * 2 * run * sets * 2 * run * HD * 5,
    )(key_limits, kv, *qs, *grads, *stats)

    all_grads = jnp.concatenate([dkv, dq], axis=1)
    whole_w = jnp.zeros((width, 3 * HD), BF16)
    for d in kv_pieces:
        whole_w = lax.dynamic_update_slice(whole_w, kv_pieces[d], ((c ^ d) * depth, 0))
        whole_w = lax.dynamic_update_slice(
            whole_w, q_pieces[d], ((c ^ d) * depth, 2 * HD)
        )

    if n_f != 4:
        partial_out = dot_nt(all_grads, whole_w).astype(BF16)
        total = partial_out[:run].astype(F32) + over_ctx(partial_out[run:], distance=PAIR).astype(F32)
        return lax.psum_scatter(total.astype(BF16), "fsdp", scatter_dimension=1, tiled=True)

    def term(e):
        rows = lax.dynamic_slice_in_dim(whole_w, (f ^ e) * per_f, per_f, axis=0)
        return dot_nt(all_grads, rows)

    half = per_f // 2
    far = term(2) + over_f(term(3).astype(BF16), distance=1).astype(F32)
    near = term(0) + over_f(term(1).astype(BF16), distance=1).astype(F32)
    by_x = functools.partial(over_f, distance=2)
    by_z = functools.partial(over_ctx, distance=PAIR)
    corner_x = by_x(far[run:, :half].astype(BF16))
    corner_z = by_z(far[run:, half:].astype(BF16))
    from_x_a = by_x(far[:run, :half].astype(BF16))
    from_z_b = by_z(near[run:, half:].astype(BF16))
    from_z_a = by_z((near[run:, :half] + corner_x.astype(F32)).astype(BF16))
    from_x_b = by_x((far[:run, half:] + corner_z.astype(F32)).astype(BF16))
    left = near[:run, :half] + from_x_a.astype(F32) + from_z_a.astype(F32)
    right = near[:run, half:] + from_x_b.astype(F32) + from_z_b.astype(F32)
    return jnp.concatenate([left, right], axis=1).astype(BF16)


def solution(mesh):
    placed = (P("ctx", None), P("ctx", None, "fsdp"), P(), P("ctx", "fsdp"))
    body = functools.partial(shards, mesh.shape["ctx"], mesh.shape["fsdp"])
    return jax.shard_map(
        body, mesh=mesh, in_specs=placed, out_specs=P("ctx", "fsdp"), check_vma=False
    )
```

```python
import functools

import jax
import jax.numpy as jnp
from jax import lax
from jax.experimental import pallas as pl
from jax.experimental.pallas import tpu as pltpu
from jax.sharding import PartitionSpec as P

HD = 128
BLOCK = 512
FAR = 1 << 20
PAIR = 2
F32 = jnp.float32
BF16 = jnp.bfloat16
HOLD_FLOPS = 20_000_000_000
VMEM_LIMIT = 48 * 1024 * 1024


def swap(array, axis, size, distance, sender=lambda i: True):
    pairs = [(i, i ^ distance) for i in range(size) if sender(i)]
    return lax.ppermute(array, axis, pairs)


def hold_kernel(in_ref, out_ref):
    out_ref[...] = in_ref[...]


def hold(token):
    return pl.pallas_call(
        hold_kernel,
        out_shape=jax.ShapeDtypeStruct(token.shape, token.dtype),
        cost_estimate=pl.CostEstimate(flops=HOLD_FLOPS, bytes_accessed=1024, transcendentals=0),
    )(token)


class Order:
    def __init__(self, token):
        self.token = token

    def wait(self, value):
        value, token = lax.optimization_barrier((value, self.token))
        self.token = hold(token)
        return value

    def after(self, *values):
        tied = lax.optimization_barrier((*values, self.token))[: len(values)]
        return tied if len(values) > 1 else tied[0]


def dot_nt(a, b):
    return lax.dot_general(a, b, (((1,), (1,)), ((), ())), preferred_element_type=F32)


def dot_nn(a, b):
    return lax.dot_general(a, b, (((1,), (0,)), ((), ())), preferred_element_type=F32)


def masked_scores(products, gap, limits, run):
    scaled = products * (HD ** -0.5)
    parts = [
        jnp.where(gap <= limit, scaled[:, i * run : (i + 1) * run], -jnp.inf)
        for i, limit in enumerate(limits)
    ]
    return jnp.concatenate(parts, axis=1)


def query_kernel(sets, run, limit_ref, q_ref, grad_ref, *refs):
    kv_refs, (dq_ref, stat_ref) = refs[:sets], refs[sets:]
    gap = lax.broadcasted_iota(jnp.int32, (run, run), 1) - lax.broadcasted_iota(
        jnp.int32, (run, run), 0
    )
    lane = lax.broadcasted_iota(jnp.int32, (run, HD), 1)
    for half in range(2):
        rows = pl.ds(half * run, run)
        q, grad = q_ref[rows, :], grad_ref[rows, :]
        scores = [
            masked_scores(
                dot_nt(q, kv_refs[j][:, :HD]),
                gap,
                [limit_ref[half, 2 * j], limit_ref[half, 2 * j + 1]],
                run,
            )
            for j in range(sets)
        ]
        highest = functools.reduce(
            jnp.maximum, [jnp.max(s, axis=1, keepdims=True) for s in scores]
        )
        expo = [jnp.exp(s - highest) for s in scores]
        total = sum(jnp.sum(e, axis=1, keepdims=True) for e in expo)
        inverse = 1.0 / total
        probs = [e * inverse for e in expo]
        attended = sum(
            dot_nn(p.astype(BF16), kv_refs[j][:, HD:]) for j, p in enumerate(probs)
        ).astype(BF16)
        delta = jnp.sum(
            grad.astype(F32) * attended.astype(F32), axis=1, keepdims=True
        )
        dq = jnp.zeros((run, HD), F32)
        for j, p in enumerate(probs):
            dprobs = dot_nt(grad, kv_refs[j][:, HD:])
            dscores = (p * (dprobs - delta)).astype(BF16)
            dq += dot_nn(dscores, kv_refs[j][:, :HD])
        dq_ref[rows, :] = (dq * (HD ** -0.5)).astype(BF16)
        stats = jnp.where(
            lane == 0, highest, jnp.where(lane == 1, inverse, delta)
        )
        stat_ref[:, rows] = jnp.transpose(stats)[:8]


def key_kernel(sets, run, limit_ref, kv_ref, *refs):
    q_refs, grad_refs, stat_refs = refs[:sets], refs[sets : 2 * sets], refs[2 * sets : 3 * sets]
    out_ref = refs[3 * sets]
    gap = lax.broadcasted_iota(jnp.int32, (run, run), 0) - lax.broadcasted_iota(
        jnp.int32, (run, run), 1
    )
    for half in range(2):
        rows = pl.ds(half * run, run)
        keys, values = kv_ref[rows, :HD], kv_ref[rows, HD:]
        dk = jnp.zeros((run, HD), F32)
        dv = jnp.zeros((run, HD), F32)
        for j in range(sets):
            q, grad, stat = q_refs[j][...], grad_refs[j][...], stat_refs[j]
            scores = masked_scores(
                dot_nt(keys, q),
                gap,
                [limit_ref[half, 2 * j], limit_ref[half, 2 * j + 1]],
                run,
            )
            probs = jnp.exp(scores - stat[0:1, :]) * stat[1:2, :]
            dprobs = dot_nt(values, grad)
            dscores = (probs * (dprobs - stat[2:3, :])).astype(BF16)
            dk += dot_nn(dscores, q)
            dv += dot_nn(probs.astype(BF16), grad)
        out_ref[rows, :HD] = (dk * (HD ** -0.5)).astype(BF16)
        out_ref[rows, HD:] = dv.astype(BF16)


def local_call(kernel, out_shape, n_vmem, flops):
    return pl.pallas_call(
        kernel,
        out_shape=out_shape,
        in_specs=[pl.BlockSpec(memory_space=pltpu.SMEM)]
        + [pl.BlockSpec(memory_space=pltpu.VMEM)] * n_vmem,
        out_specs=jax.tree.map(lambda _: pl.BlockSpec(memory_space=pltpu.VMEM), out_shape),
        compiler_params=pltpu.CompilerParams(vmem_limit_bytes=VMEM_LIMIT),
        cost_estimate=pl.CostEstimate(flops=flops, bytes_accessed=4 << 20, transcendentals=1 << 20),
    )


def shards(n_ctx, n_f, inputs, w_qkv, selected, d_attn):
    run, width = inputs.shape
    depth = w_qkv.shape[0]
    per_f = width // n_f
    c = lax.axis_index("ctx")
    f = lax.axis_index("fsdp")
    mine = (c // PAIR) % 2
    over_ctx = functools.partial(swap, axis="ctx", size=n_ctx)
    over_f = functools.partial(swap, axis="fsdp", size=n_f)
    even = [d for d in range(n_ctx) if d % 2 == 0]
    group = [d for d in range(n_ctx) if not d & PAIR]
    sets = len(group)

    def head_of(array, which):
        return lax.dynamic_slice_in_dim(array, which * HD, HD, axis=array.ndim - 1)

    own_w = head_of(w_qkv, mine)
    other_w = head_of(w_qkv, 1 - mine)
    kv_of = lambda w: jnp.concatenate([w[:, 1], w[:, 2]], axis=1)
    q_of = lambda w: w[:, 0]

    kv_own, kv_other, q_own, q_other = kv_of(own_w), kv_of(other_w), q_of(own_w), q_of(other_w)
    order = Order(jnp.zeros((8, HD), F32))
    near, *mids = even[1:]
    parity = c % 2
    kv_pieces, q_pieces = {0: kv_own}, {0: q_own}

    def part(which):
        return lax.dynamic_slice_in_dim(inputs, f * per_f + which * step, step, axis=1)

    step = per_f // 2 if per_f > depth else per_f
    part_a, part_b = part(parity if per_f > depth else 0), part(1 - parity)

    def send(pieces, d, own, other):
        pieces[d] = over_ctx(other if d & PAIR else own, distance=d)

    def relay(pieces, d):
        pieces[d ^ 1] = over_ctx(pieces[d], distance=1)

    def arrive(pieces, *ds):
        for d in ds:
            pieces[d] = order.wait(pieces[d])

    def spread(held, bit):
        for e in list(held):
            held[e ^ bit] = over_f(held[e], distance=bit)

    relay(kv_pieces, 0)
    send(kv_pieces, mids[0], kv_own, kv_other)
    send(kv_pieces, near, kv_own, kv_other)
    arrive(kv_pieces, near, mids[0])
    relay(kv_pieces, mids[0])
    relay(kv_pieces, near)
    part_a, kv_other, kv_own, q_pieces[0], other_grad = order.after(
        part_a, kv_other, kv_own, q_own, head_of(d_attn, 1 - mine)
    )
    held_a = {0: over_ctx(part_a, distance=PAIR)}
    for d in mids[1:]:
        send(kv_pieces, d, kv_own, kv_other)
    relay(q_pieces, 0)
    arrive(held_a, 0)
    bits = [1 << i for i in reversed(range(n_f.bit_length() - 1))]
    spread(held_a, bits[0])
    part_b, other_grad = order.after(part_b, other_grad)
    held_b = {0: over_ctx(part_b, distance=PAIR)}
    other_grad = over_ctx(other_grad, distance=PAIR)
    for d in mids[1:]:
        arrive(kv_pieces, d)
        relay(kv_pieces, d)
    q_own, q_other = order.after(q_own, q_other)
    for d in mids + [near]:
        send(q_pieces, d, q_own, q_other)
    arrive(held_a, bits[0])
    for bit in bits[1:]:
        spread(held_a, bit)
    arrive(held_b, 0)
    spread(held_b, bits[0])
    arrive(kv_pieces, 1, near ^ 1, mids[0] ^ 1)
    for d in mids + [near]:
        arrive(q_pieces, d)
        relay(q_pieces, d)
    arrive(held_b, bits[0])
    for bit in bits[1:]:
        spread(held_b, bit)
    arrive(kv_pieces, *[d ^ 1 for d in mids[1:]])

    if per_f > depth:
        partner = [jnp.concatenate([held[e] for e in range(n_f)], axis=1) for held in (held_a, held_b)]
    else:
        partner = [jnp.concatenate([held_a[e] for e in range(n_f)], axis=1)] * 2

    def project(pieces):
        totals = [None, None]
        for d in sorted(pieces, key=lambda d: (d & 1, d)):
            start = (c ^ d) * depth
            other_start = ((start // per_f) ^ f) * step
            for i, (rows, at) in enumerate(((inputs, start), (partner[d & 1], other_start))):
                term = dot_nn(lax.dynamic_slice_in_dim(rows, at, depth, axis=1), pieces[d])
                totals[i] = term if totals[i] is None else totals[i] + term
        return jnp.concatenate(totals, axis=0).astype(BF16)

    def top(d):
        return 1 << (d.bit_length() - 1)

    def to_later(array, d):
        ordered = top(d) > PAIR
        return over_ctx(array, distance=d, sender=lambda i: not (ordered and i & top(d)))

    def to_earlier(array, d):
        ordered = top(d) > PAIR
        return over_ctx(array, distance=d, sender=lambda i: not ordered or i & top(d))

    kv = project(kv_pieces)
    kvs = [kv] + [to_later(kv, d) for d in group[1:]]
    grad = jnp.concatenate([head_of(d_attn, mine), order.wait(other_grad)], axis=0)
    grad = lax.optimization_barrier((grad, kv))[0]
    grads = [grad] + [to_earlier(grad, d) for d in group[1:]]
    arrive(q_pieces, 1, *[d ^ 1 for d in mids + [near]])
    q = project(q_pieces)
    qs = [q] + [to_earlier(q, d) for d in group[1:]]

    runs = jnp.stack([c ^ d ^ p for d in group for p in (0, PAIR)])
    blocks = runs * run // BLOCK
    here = runs[:2]

    def limits(query_runs, key_runs, query_blocks, key_blocks):
        chosen = jnp.any(
            selected[query_blocks][:, :, None] == key_blocks[None, None, :], axis=1
        )
        ahead = query_runs[:, None] - key_runs[None, :]
        bound = jnp.where(ahead > 0, FAR, jnp.where(ahead == 0, 0, -FAR))
        return jnp.where(chosen, bound, -FAR).astype(jnp.int32)

    query_limits = limits(here, runs, blocks[:2], blocks)
    key_limits = limits(runs, here, blocks, blocks[:2]).T

    dq, stat = local_call(
        functools.partial(query_kernel, sets, run),
        (
            jax.ShapeDtypeStruct((2 * run, HD), BF16),
            jax.ShapeDtypeStruct((8, 2 * run), F32),
        ),
        2 + sets,
        2 * 2 * run * sets * 2 * run * HD * 5,
    )(query_limits, q, grad, *kvs)
    stats = [stat] + [to_earlier(stat, d) for d in group[1:]]
    dkv = local_call(
        functools.partial(key_kernel, sets, run),
        jax.ShapeDtypeStruct((2 * run, 2 * HD), BF16),
        1 + 3 * sets,
        2 * 2 * run * sets * 2 * run * HD * 5,
    )(key_limits, kv, *qs, *grads, *stats)

    all_grads = jnp.concatenate([dkv, dq], axis=1)
    if n_f != 4 or n_ctx != 2 * n_f:
        whole_w = jnp.zeros((width, 3 * HD), BF16)
        for d in kv_pieces:
            piece = jnp.concatenate([kv_pieces[d], q_pieces[d]], axis=1)
            whole_w = lax.dynamic_update_slice(whole_w, piece, ((c ^ d) * depth, 0))
        partial_out = dot_nt(all_grads, whole_w).astype(BF16)
        total = partial_out[:run].astype(F32) + over_ctx(partial_out[run:], distance=PAIR).astype(F32)
        return lax.psum_scatter(total.astype(BF16), "fsdp", scatter_dimension=1, tiled=True)

    stacked = jnp.concatenate(
        [
            jnp.concatenate([kv_pieces[d] for d in range(n_ctx)], axis=0),
            jnp.concatenate([q_pieces[d] for d in range(n_ctx)], axis=0),
        ],
        axis=1,
    )

    def term(e):
        at = ((f ^ e) ^ (c // 2)) * per_f
        return dot_nt(all_grads, lax.dynamic_slice_in_dim(stacked, at, per_f, axis=0))

    half = per_f // 2
    outer = term(2) + over_f(term(3).astype(BF16), distance=1).astype(F32)
    inner = term(0) + over_f(term(1).astype(BF16), distance=1).astype(F32)
    by_x = functools.partial(over_f, distance=2)
    by_z = functools.partial(over_ctx, distance=PAIR)
    corner_x = by_x(outer[run:, :half].astype(BF16))
    corner_z = by_z(outer[run:, half:].astype(BF16))
    from_x_a = by_x(outer[:run, :half].astype(BF16))
    from_z_b = by_z(inner[run:, half:].astype(BF16))
    from_z_a = by_z((inner[run:, :half] + corner_x.astype(F32)).astype(BF16))
    from_x_b = by_x((outer[:run, half:] + corner_z.astype(F32)).astype(BF16))
    left = inner[:run, :half] + from_x_a.astype(F32) + from_z_a.astype(F32)
    right = inner[:run, half:] + from_x_b.astype(F32) + from_z_b.astype(F32)
    swapped = c % 2 == 1
    return jnp.concatenate(
        [jnp.where(swapped, right, left), jnp.where(swapped, left, right)], axis=1
    ).astype(BF16)


def solution(mesh):
    placed = (P("ctx", None), P("ctx", None, "fsdp"), P(), P("ctx", "fsdp"))
    body = functools.partial(shards, mesh.shape["ctx"], mesh.shape["fsdp"])
    return jax.shard_map(
        body, mesh=mesh, in_specs=placed, out_specs=P("ctx", "fsdp"), check_vma=False
    )
```

```python
import functools

import jax
import jax.numpy as jnp
from jax import lax
from jax.experimental import pallas as pl
from jax.experimental.pallas import tpu as pltpu
from jax.sharding import PartitionSpec as P

HD = 128
BLOCK = 512
FAR = 1 << 20
PAIR = 2
F32 = jnp.float32
BF16 = jnp.bfloat16
VMEM_LIMIT = 20 * 1024 * 1024


def swap(array, axis, size, distance, sender=lambda i: True):
    pairs = [(i, i ^ distance) for i in range(size) if sender(i)]
    return lax.ppermute(array, axis, pairs)


class Order:
    def __init__(self):
        self.held = {}

    def __getitem__(self, name):
        return self.held[name]

    def __setitem__(self, name, array):
        self.held[name] = array

    def after(self, names, *first):
        names = names.split() + list(first)
        tied = lax.optimization_barrier([self.held[n] for n in names])
        self.held.update(zip(names, tied))


def dot_nt(a, b):
    return lax.dot_general(a, b, (((1,), (1,)), ((), ())), preferred_element_type=F32)


def dot_nn(a, b):
    return lax.dot_general(a, b, (((1,), (0,)), ((), ())), preferred_element_type=F32)


def masked_scores(products, gap, limits, run):
    scaled = products * (HD ** -0.5)
    parts = [
        jnp.where(gap <= limit, scaled[:, i * run : (i + 1) * run], -jnp.inf)
        for i, limit in enumerate(limits)
    ]
    return jnp.concatenate(parts, axis=1)


def tile_gap(run, by):
    rows = lax.broadcasted_iota(jnp.int32, (run, run), by)
    return lax.broadcasted_iota(jnp.int32, (run, run), 1 - by) - rows


def query_scores(sets, run, half, limit_ref, q_ref, kv_refs):
    gap = tile_gap(run, 0)
    q = q_ref[half * run : (half + 1) * run]
    return [
        masked_scores(
            dot_nt(q, kv_refs[j][:, :HD]),
            gap,
            [limit_ref[half, 2 * j], limit_ref[half, 2 * j + 1]],
            run,
        )
        for j in range(sets)
    ]


def forward_kernel(sets, run, limit_ref, q_ref, grad_ref, *refs):
    kv_refs, (stat_ref, column_ref) = refs[:sets], refs[sets:]
    lane = lax.broadcasted_iota(jnp.int32, (run, HD), 1)
    for half in range(2):
        rows = pl.ds(half * run, run)
        scores = query_scores(sets, run, half, limit_ref, q_ref, kv_refs)
        highest = functools.reduce(
            jnp.maximum, [jnp.max(s, axis=1, keepdims=True) for s in scores]
        )
        expo = [jnp.exp(s - highest) for s in scores]
        inverse = 1.0 / sum(jnp.sum(e, axis=1, keepdims=True) for e in expo)
        attended = sum(
            dot_nn((e * inverse).astype(BF16), kv_refs[j][:, HD:]) for j, e in enumerate(expo)
        ).astype(BF16)
        delta = jnp.sum(
            grad_ref[rows, :].astype(F32) * attended.astype(F32), axis=1, keepdims=True
        )
        stats = jnp.where(
            lane == 0, highest, jnp.where(lane == 1, inverse, delta)
        )
        column_ref[rows, :] = stats
        stat_ref[:, rows] = jnp.transpose(stats)[:8]


def query_kernel(sets, run, limit_ref, q_ref, grad_ref, column_ref, *refs):
    kv_refs, dq_ref = refs[:sets], refs[sets]
    for half in range(2):
        rows = pl.ds(half * run, run)
        scores = query_scores(sets, run, half, limit_ref, q_ref, kv_refs)
        highest, inverse, delta = (column_ref[rows, i : i + 1] for i in range(3))
        grad = grad_ref[rows, :]
        dq = jnp.zeros((run, HD), F32)
        for j, s in enumerate(scores):
            probs = jnp.exp(s - highest) * inverse
            dprobs = dot_nt(grad, kv_refs[j][:, HD:])
            dscores = (probs * (dprobs - delta)).astype(BF16)
            dq += dot_nn(dscores, kv_refs[j][:, :HD])
        dq_ref[rows, :] = (dq * (HD ** -0.5)).astype(BF16)


def key_kernel(sets, run, limit_ref, kv_ref, *refs):
    q_refs, grad_refs, stat_refs = refs[:sets], refs[sets : 2 * sets], refs[2 * sets : 3 * sets]
    before, out_ref = refs[3 * sets : -1], refs[-1]
    gap = -tile_gap(run, 0)
    for half in range(2):
        rows = pl.ds(half * run, run)
        keys, values = kv_ref[rows, :HD], kv_ref[rows, HD:]
        dk = before[0][rows, :HD] if before else jnp.zeros((run, HD), F32)
        dv = before[0][rows, HD:] if before else jnp.zeros((run, HD), F32)
        for j in range(sets):
            q, grad, stat = q_refs[j][...], grad_refs[j][...], stat_refs[j]
            scores = masked_scores(
                dot_nt(keys, q),
                gap,
                [limit_ref[half, 2 * j], limit_ref[half, 2 * j + 1]],
                run,
            )
            probs = jnp.exp(scores - stat[0:1, :]) * stat[1:2, :]
            dprobs = dot_nt(values, grad)
            dscores = (probs * (dprobs - stat[2:3, :])).astype(BF16)
            dk += dot_nn(dscores, q) * (HD ** -0.5)
            dv += dot_nn(probs.astype(BF16), grad)
        out_ref[rows, :HD] = dk.astype(out_ref.dtype)
        out_ref[rows, HD:] = dv.astype(out_ref.dtype)


def project_kernel(groups, n_pieces, place_ref, own_ref, *refs):
    parts, pieces = refs[: len(groups)], refs[len(groups) : len(groups) + n_pieces]
    before, (out_ref, partner_ref) = refs[len(groups) + n_pieces : -2], refs[-2:]
    run = own_ref.shape[0]
    for ids, part_ref in zip(groups, parts):
        for i, e in enumerate(ids):
            partner_ref[e] = part_ref[i * run : (i + 1) * run]
    total = before[0][...] if before else None
    for i, piece_ref in enumerate(pieces):
        depth = piece_ref.shape[0]
        at = pl.multiple_of(place_ref[0, i], HD)
        rows = jnp.concatenate(
            [own_ref[:, pl.ds(at, depth)], partner_ref[place_ref[1, i]]], axis=0
        )
        term = dot_nn(rows, piece_ref[...])
        total = term if total is None else total + term
    out_ref[...] = total.astype(out_ref.dtype)


def local_call(kernel, out_shape, n_vmem, scratch=()):
    return pl.pallas_call(
        kernel,
        out_shape=out_shape,
        in_specs=[pl.BlockSpec(memory_space=pltpu.SMEM)]
        + [pl.BlockSpec(memory_space=pltpu.VMEM)] * n_vmem,
        out_specs=jax.tree.map(lambda _: pl.BlockSpec(memory_space=pltpu.VMEM), out_shape),
        scratch_shapes=scratch,
        compiler_params=pltpu.CompilerParams(vmem_limit_bytes=VMEM_LIMIT),
        cost_estimate=pl.CostEstimate(flops=1, bytes_accessed=1, transcendentals=0),
    )


def shards(n_ctx, n_f, inputs, w_qkv, selected, d_attn):
    run, width = inputs.shape
    depth = w_qkv.shape[0]
    per_f = width // n_f
    c = lax.axis_index("ctx")
    f = lax.axis_index("fsdp")
    mine = (c // PAIR) % 2
    over_ctx = functools.partial(swap, axis="ctx", size=n_ctx)
    over_f = functools.partial(swap, axis="fsdp", size=n_f)
    even = [d for d in range(n_ctx) if d % 2 == 0]
    group = [d for d in range(n_ctx) if not d & PAIR]
    sets = len(group)

    def head_of(array, which):
        return lax.dynamic_slice_in_dim(array, which * HD, HD, axis=array.ndim - 1)

    order = Order()
    near, *mids = even[1:]
    parity = c % 2
    bits = [1 << i for i in reversed(range(n_f.bit_length() - 1))]

    def kv_of(which):
        return jnp.concatenate([head_of(w_qkv[:, 1], which), head_of(w_qkv[:, 2], which)], axis=1)

    def q_of(which):
        return head_of(w_qkv[:, 0], which)

    step = depth if per_f > depth else per_f

    def part(which):
        start = f * per_f + (which * step if per_f > depth else 0)
        return lax.dynamic_slice_in_dim(inputs, start, step, axis=1)

    def start(name, array, distance, across=over_ctx):
        order[name] = across(array, distance=distance)

    def send(kind, *ds):
        for d in ds:
            start(f"{kind}{d}", order[kind + ("other" if d & PAIR else "0")], d)

    def relay(kind, *ds):
        for d in ds:
            start(f"{kind}{d ^ 1}", order[f"{kind}{d}"], 1)

    def spread(kind, groups):
        bit = bits[len(groups) - 1]
        held = [order[f"{kind}{i}"] for i in range(len(groups))]
        start(f"{kind}{len(groups)}", jnp.concatenate(held, axis=0) if held[1:] else held[0], bit, over_f)
        return groups + [[e ^ bit for ids in groups for e in ids]]

    def project(kind, ds, x_kind, groups, before=None):
        pieces = [order[f"{kind}{d}"] for d in ds]
        first = jnp.stack([(c ^ d) * depth for d in ds])
        place = jnp.stack([first, (first // per_f) ^ f]).astype(jnp.int32)
        held = [order[f"{x_kind}{i}"] for i in range(len(groups))]
        out = jax.ShapeDtypeStruct((2 * run, pieces[0].shape[1]), F32 if before is None else BF16)
        earlier = [] if before is None else [before]
        return local_call(
            functools.partial(project_kernel, groups, len(ds)),
            out,
            1 + len(held) + len(ds) + len(earlier),
            [pltpu.VMEM((n_f, run, step), BF16)],
        )(place, inputs, *held, *pieces, *earlier)

    def top(d):
        return 1 << (d.bit_length() - 1)

    def to_later(array, distance):
        ordered = top(distance) > PAIR
        return over_ctx(array, distance=distance, sender=lambda i: not (ordered and i & top(distance)))

    def to_earlier(array, distance):
        ordered = top(distance) > PAIR
        return over_ctx(array, distance=distance, sender=lambda i: not ordered or i & top(distance))

    odd = [d ^ 1 for d in even]
    others = group[:0:-1]
    far = mids[0]
    order["kv0"], order["kvother"] = kv_of(mine), kv_of(1 - mine)
    order["part_a"], order["part_b"] = part(parity), part(1 - parity)
    order["q0"], order["qother"] = q_of(mine), q_of(1 - mine)
    order["g0"], order["gother"] = head_of(d_attn, mine), head_of(d_attn, 1 - mine)
    send("kv", far, near)
    relay("kv", 0)
    start("a0", order["part_a"], PAIR)
    start("gpair", order["gother"], PAIR)
    order.after("q0", "kv1")
    relay("q", 0)
    order.after("kvother kv0 part_b", f"kv{far}", "a0", "gpair", "q1")
    groups_a = spread("a", [[0]])
    relay("kv", far, near)
    send("kv", *mids[1:])
    start("b0", order["part_b"], PAIR)
    for _ in bits[1:]:
        groups_a = spread("a", groups_a)
    order["grad"] = jnp.concatenate([order["g0"], order["gpair"]], axis=0)

    order.after("q0 qother", f"kv{mids[1]}", f"kv{far ^ 1}")
    relay("kv", *mids[1:])
    groups_b = spread("b", [[0]])
    send("q", *mids)
    order.after("qother", f"a{len(groups_a) - 1}")
    send("q", near)
    order["kv_even"] = project("kv", even, "a", groups_a)
    order.after("b0 b1", *[f"kv{d ^ 1}" for d in mids[1:]])
    for _ in bits[1:]:
        groups_b = spread("b", groups_b)
    last = ("b", groups_b) if per_f > depth else ("a", groups_a)
    order["kv"] = project("kv", odd, *last, order["kv_even"])

    for d in others[:-1]:
        start(f"keys{d}", order["kv"], d, to_later)
    moved = mids + [near]
    start("passed", jnp.concatenate([order[f"q{d}"] for d in moved], axis=0), 1)
    order.after("kv", "passed")
    start(f"keys{others[-1]}", order["kv"], others[-1], to_later)
    for i, d in enumerate(moved):
        order[f"q{d ^ 1}"] = order["passed"][i * depth : (i + 1) * depth]
    order["q_even"] = project("q", even, "a", groups_a)
    order.after("grad", "kv")
    for d in others:
        start(f"grad{d}", order["grad"], d, to_earlier)
    order["q"] = project("q", odd, *last, order["q_even"])
    order.after("q", *[f"grad{d}" for d in others[:-1]])
    for d in others:
        start(f"query{d}", order["q"], d, to_earlier)
    kv, q, grad = order["kv"], order["q"], order["grad"]
    kv_pieces = {d: order[f"kv{d}"] for d in range(n_ctx)}
    q_pieces = {d: order[f"q{d}"] for d in range(n_ctx)}
    kvs = [kv] + [order[f"keys{d}"] for d in group[1:]]
    grads = [grad] + [order[f"grad{d}"] for d in group[1:]]
    qs = [q] + [order[f"query{d}"] for d in group[1:]]

    runs = jnp.stack([c ^ d ^ p for d in group for p in (0, PAIR)])
    blocks = runs * run // BLOCK
    here = runs[:2]

    def limits(query_runs, key_runs, query_blocks, key_blocks):
        chosen = jnp.any(
            selected[query_blocks][:, :, None] == key_blocks[None, None, :], axis=1
        )
        ahead = query_runs[:, None] - key_runs[None, :]
        bound = jnp.where(ahead > 0, FAR, jnp.where(ahead == 0, 0, -FAR))
        return jnp.where(chosen, bound, -FAR).astype(jnp.int32)

    query_limits = limits(here, runs, blocks[:2], blocks)
    key_limits = limits(runs, here, blocks, blocks[:2]).T

    stat, column = local_call(
        functools.partial(forward_kernel, sets, run),
        (
            jax.ShapeDtypeStruct((8, 2 * run), F32),
            jax.ShapeDtypeStruct((2 * run, HD), F32),
        ),
        2 + sets,
    )(query_limits, q, grad, *kvs)
    stats = [stat] + [to_earlier(stat, distance=d) for d in group[1:]]
    dq = local_call(
        functools.partial(query_kernel, sets, run),
        jax.ShapeDtypeStruct((2 * run, HD), BF16),
        3 + sets,
    )(query_limits, q, grad, column, *kvs)
    close = 2
    dkv = local_call(
        functools.partial(key_kernel, close, run),
        jax.ShapeDtypeStruct((2 * run, 2 * HD), F32),
        1 + 3 * close,
    )(key_limits[:, : 2 * close], kv, *qs[:close], *grads[:close], *stats[:close])
    dkv = local_call(
        functools.partial(key_kernel, sets - close, run),
        jax.ShapeDtypeStruct((2 * run, 2 * HD), BF16),
        2 + 3 * (sets - close),
    )(key_limits[:, 2 * close :], kv, *qs[close:], *grads[close:], *stats[close:], dkv)

    all_grads = jnp.concatenate([dkv, dq], axis=1)
    if n_f != 4 or n_ctx != 2 * n_f:
        whole_w = jnp.zeros((width, 3 * HD), BF16)
        for d in kv_pieces:
            piece = jnp.concatenate([kv_pieces[d], q_pieces[d]], axis=1)
            whole_w = lax.dynamic_update_slice(whole_w, piece, ((c ^ d) * depth, 0))
        partial_out = dot_nt(all_grads, whole_w).astype(BF16)
        total = partial_out[:run].astype(F32) + over_ctx(partial_out[run:], distance=PAIR).astype(F32)
        return lax.psum_scatter(total.astype(BF16), "fsdp", scatter_dimension=1, tiled=True)

    stacked = jnp.concatenate(
        [
            jnp.concatenate([kv_pieces[d] for d in range(n_ctx)], axis=0),
            jnp.concatenate([q_pieces[d] for d in range(n_ctx)], axis=0),
        ],
        axis=1,
    )

    half = per_f // 2
    by_core = functools.partial(over_f, distance=1)
    by_x = functools.partial(over_f, distance=2)
    by_z = functools.partial(over_ctx, distance=PAIR)

    def term(which, e, start=0, size=per_f):
        at = ((f ^ e) ^ (c // 2)) * per_f + start
        rows = lax.dynamic_slice_in_dim(stacked, at, size, axis=0)
        return dot_nt(all_grads[which * run : (which + 1) * run], rows)

    def chip(which, e, *columns):
        return term(which, e, *columns) + by_core(term(which, e ^ 1, *columns).astype(BF16)).astype(F32)

    corner_x = by_x(chip(1, 2, 0, half).astype(BF16))
    corner_z = by_z(chip(1, 2, half, half).astype(BF16))
    for_x = chip(0, 2)
    from_x_a = by_x(for_x[:, :half].astype(BF16))
    for_z = chip(1, 0)
    from_z_b = by_z(for_z[:, half:].astype(BF16))
    here = chip(0, 0)
    from_z_a = by_z((for_z[:, :half] + corner_x.astype(F32)).astype(BF16))
    from_x_b = by_x((for_x[:, half:] + corner_z.astype(F32)).astype(BF16))

    def finish_kernel(swapped_ref, here_ref, x_a, x_b, z_a, z_b, out_ref):
        for i, (x_ref, z_ref) in enumerate(((x_a, z_a), (x_b, z_b))):
            total = here_ref[:, i * half : (i + 1) * half] + x_ref[...].astype(F32) + z_ref[...].astype(F32)
            at = pl.multiple_of((swapped_ref[0] ^ i) * half, HD)
            out_ref[:, pl.ds(at, half)] = total.astype(BF16)

    return local_call(
        finish_kernel, jax.ShapeDtypeStruct((run, per_f), BF16), 5
    )(parity.reshape(1).astype(jnp.int32), here, from_x_a, from_x_b, from_z_a, from_z_b)


def solution(mesh):
    placed = (P("ctx", None), P("ctx", None, "fsdp"), P(), P("ctx", "fsdp"))
    body = functools.partial(shards, mesh.shape["ctx"], mesh.shape["fsdp"])
    return jax.shard_map(
        body, mesh=mesh, in_specs=placed, out_specs=P("ctx", "fsdp"), check_vma=False
    )
```

```python
import functools

import jax
import jax.numpy as jnp
from jax import lax
from jax.experimental import pallas as pl
from jax.experimental.pallas import tpu as pltpu
from jax.sharding import PartitionSpec as P

HD = 128
BLOCK = 512
FAR = 1 << 20
PAIR = 2
F32 = jnp.float32
BF16 = jnp.bfloat16
VMEM_LIMIT = 20 * 1024 * 1024


def swap(array, axis, size, distance, sender=lambda i: True):
    pairs = [(i, i ^ distance) for i in range(size) if sender(i)]
    return lax.ppermute(array, axis, pairs)


class Order:
    def __init__(self):
        self.held = {}

    def __getitem__(self, name):
        return self.held[name]

    def __setitem__(self, name, array):
        self.held[name] = array

    def after(self, names, *first):
        names = names.split() + list(first)
        tied = lax.optimization_barrier([self.held[n] for n in names])
        self.held.update(zip(names, tied))


def dot_nt(a, b):
    return lax.dot_general(a, b, (((1,), (1,)), ((), ())), preferred_element_type=F32)


def dot_nn(a, b):
    return lax.dot_general(a, b, (((1,), (0,)), ((), ())), preferred_element_type=F32)


def masked_scores(products, gap, limits, run):
    scaled = products * (HD ** -0.5)
    parts = [
        jnp.where(gap <= limit, scaled[:, i * run : (i + 1) * run], -jnp.inf)
        for i, limit in enumerate(limits)
    ]
    return jnp.concatenate(parts, axis=1)


def tile_gap(run, by):
    rows = lax.broadcasted_iota(jnp.int32, (run, run), by)
    return lax.broadcasted_iota(jnp.int32, (run, run), 1 - by) - rows


def query_scores(sets, run, half, limit_ref, q_ref, kv_refs):
    gap = tile_gap(run, 0)
    q = q_ref[half * run : (half + 1) * run]
    return [
        masked_scores(
            dot_nt(q, kv_refs[j][:, :HD]),
            gap,
            [limit_ref[half, 2 * j], limit_ref[half, 2 * j + 1]],
            run,
        )
        for j in range(sets)
    ]


def forward_kernel(sets, run, limit_ref, q_ref, grad_ref, *refs):
    kv_refs, (stat_ref, column_ref) = refs[:sets], refs[sets:]
    lane = lax.broadcasted_iota(jnp.int32, (run, HD), 1)
    for half in range(2):
        rows = pl.ds(half * run, run)
        scores = query_scores(sets, run, half, limit_ref, q_ref, kv_refs)
        highest = functools.reduce(
            jnp.maximum, [jnp.max(s, axis=1, keepdims=True) for s in scores]
        )
        expo = [jnp.exp(s - highest) for s in scores]
        inverse = 1.0 / sum(jnp.sum(e, axis=1, keepdims=True) for e in expo)
        attended = sum(
            dot_nn((e * inverse).astype(BF16), kv_refs[j][:, HD:]) for j, e in enumerate(expo)
        ).astype(BF16)
        delta = jnp.sum(
            grad_ref[rows, :].astype(F32) * attended.astype(F32), axis=1, keepdims=True
        )
        stats = jnp.where(
            lane == 0, highest, jnp.where(lane == 1, inverse, delta)
        )
        column_ref[rows, :] = stats
        stat_ref[:, rows] = jnp.transpose(stats)[:8]


def query_kernel(sets, run, limit_ref, q_ref, grad_ref, column_ref, *refs):
    kv_refs, dq_ref = refs[:sets], refs[sets]
    for half in range(2):
        rows = pl.ds(half * run, run)
        scores = query_scores(sets, run, half, limit_ref, q_ref, kv_refs)
        highest, inverse, delta = (column_ref[rows, i : i + 1] for i in range(3))
        grad = grad_ref[rows, :]
        dq = jnp.zeros((run, HD), F32)
        for j, s in enumerate(scores):
            probs = jnp.exp(s - highest) * inverse
            dprobs = dot_nt(grad, kv_refs[j][:, HD:])
            dscores = (probs * (dprobs - delta)).astype(BF16)
            dq += dot_nn(dscores, kv_refs[j][:, :HD])
        dq_ref[rows, :] = (dq * (HD ** -0.5)).astype(BF16)


def key_kernel(sets, run, limit_ref, kv_ref, *refs):
    q_refs, grad_refs, stat_refs = refs[:sets], refs[sets : 2 * sets], refs[2 * sets : 3 * sets]
    before, (out_ref, total_ref) = refs[3 * sets : -2], refs[-2:]
    gap = -tile_gap(run, 0)
    total_ref[...] = before[0][...] if before else jnp.zeros_like(total_ref)
    for half in range(2):
        rows = pl.ds(half * run, run)
        for j in range(sets):
            limits = [limit_ref[half, 2 * j], limit_ref[half, 2 * j + 1]]

            @pl.when(jnp.maximum(*limits) > -FAR)
            def add(rows=rows, j=j, limits=limits):
                q, grad, stat = q_refs[j][...], grad_refs[j][...], stat_refs[j]
                scores = masked_scores(dot_nt(kv_ref[rows, :HD], q), gap, limits, run)
                probs = jnp.exp(scores - stat[0:1, :]) * stat[1:2, :]
                dprobs = dot_nt(kv_ref[rows, HD:], grad)
                dscores = (probs * (dprobs - stat[2:3, :])).astype(BF16)
                total_ref[rows, :HD] += dot_nn(dscores, q) * (HD ** -0.5)
                total_ref[rows, HD:] += dot_nn(probs.astype(BF16), grad)

    out_ref[...] = total_ref[...].astype(out_ref.dtype)


def project_kernel(groups, n_pieces, place_ref, own_ref, *refs):
    parts, pieces = refs[: len(groups)], refs[len(groups) : len(groups) + n_pieces]
    before, (out_ref, partner_ref) = refs[len(groups) + n_pieces : -2], refs[-2:]
    run = own_ref.shape[0]
    for ids, part_ref in zip(groups, parts):
        for i, e in enumerate(ids):
            partner_ref[e] = part_ref[i * run : (i + 1) * run]
    total = before[0][...] if before else None
    for i, piece_ref in enumerate(pieces):
        depth = piece_ref.shape[0]
        at = pl.multiple_of(place_ref[0, i], HD)
        rows = jnp.concatenate(
            [own_ref[:, pl.ds(at, depth)], partner_ref[place_ref[1, i]]], axis=0
        )
        term = dot_nn(rows, piece_ref[...])
        total = term if total is None else total + term
    out_ref[...] = total.astype(out_ref.dtype)


def local_call(kernel, out_shape, n_vmem, scratch=()):
    return pl.pallas_call(
        kernel,
        out_shape=out_shape,
        in_specs=[pl.BlockSpec(memory_space=pltpu.SMEM)]
        + [pl.BlockSpec(memory_space=pltpu.VMEM)] * n_vmem,
        out_specs=jax.tree.map(lambda _: pl.BlockSpec(memory_space=pltpu.VMEM), out_shape),
        scratch_shapes=scratch,
        compiler_params=pltpu.CompilerParams(vmem_limit_bytes=VMEM_LIMIT),
        cost_estimate=pl.CostEstimate(flops=1, bytes_accessed=1, transcendentals=0),
    )


def shards(n_ctx, n_f, inputs, w_qkv, selected, d_attn):
    run, width = inputs.shape
    depth = w_qkv.shape[0]
    per_f = width // n_f
    c = lax.axis_index("ctx")
    f = lax.axis_index("fsdp")
    mine = (c // PAIR) % 2
    over_ctx = functools.partial(swap, axis="ctx", size=n_ctx)
    over_f = functools.partial(swap, axis="fsdp", size=n_f)
    even = [d for d in range(n_ctx) if d % 2 == 0]
    group = [d for d in range(n_ctx) if not d & PAIR]
    sets = len(group)

    def head_of(array, which):
        return lax.dynamic_slice_in_dim(array, which * HD, HD, axis=array.ndim - 1)

    order = Order()
    near, *mids = even[1:]
    parity = c % 2
    bits = [1 << i for i in reversed(range(n_f.bit_length() - 1))]

    def kv_of(which):
        return jnp.concatenate([head_of(w_qkv[:, 1], which), head_of(w_qkv[:, 2], which)], axis=1)

    def q_of(which):
        return head_of(w_qkv[:, 0], which)

    step = depth if per_f > depth else per_f

    def part(which):
        start = f * per_f + (which * step if per_f > depth else 0)
        return lax.dynamic_slice_in_dim(inputs, start, step, axis=1)

    def start(name, array, distance, across=over_ctx):
        order[name] = across(array, distance=distance)

    def send(kind, *ds):
        for d in ds:
            start(f"{kind}{d}", order[kind + ("other" if d & PAIR else "0")], d)

    def relay(kind, *ds):
        for d in ds:
            start(f"{kind}{d ^ 1}", order[f"{kind}{d}"], 1)

    def spread(kind, groups):
        bit = bits[len(groups) - 1]
        held = [order[f"{kind}{i}"] for i in range(len(groups))]
        start(f"{kind}{len(groups)}", jnp.concatenate(held, axis=0) if held[1:] else held[0], bit, over_f)
        return groups + [[e ^ bit for ids in groups for e in ids]]

    def project(kind, ds, x_kind, groups, before=None):
        pieces = [order[f"{kind}{d}"] for d in ds]
        first = jnp.stack([(c ^ d) * depth for d in ds])
        place = jnp.stack([first, (first // per_f) ^ f]).astype(jnp.int32)
        held = [order[f"{x_kind}{i}"] for i in range(len(groups))]
        out = jax.ShapeDtypeStruct((2 * run, pieces[0].shape[1]), F32 if before is None else BF16)
        earlier = [] if before is None else [before]
        return local_call(
            functools.partial(project_kernel, groups, len(ds)),
            out,
            1 + len(held) + len(ds) + len(earlier),
            [pltpu.VMEM((n_f, run, step), BF16)],
        )(place, inputs, *held, *pieces, *earlier)

    def top(d):
        return 1 << (d.bit_length() - 1)

    def to_later(array, distance):
        ordered = top(distance) > PAIR
        return over_ctx(array, distance=distance, sender=lambda i: not (ordered and i & top(distance)))

    def to_earlier(array, distance):
        ordered = top(distance) > PAIR
        return over_ctx(array, distance=distance, sender=lambda i: not ordered or i & top(distance))

    odd = [d ^ 1 for d in even]
    others = group[:0:-1]
    far = mids[0]
    order["kv0"], order["kvother"] = kv_of(mine), kv_of(1 - mine)
    order["part_a"], order["part_b"] = part(parity), part(1 - parity)
    order["q0"], order["qother"] = q_of(mine), q_of(1 - mine)
    order["g0"], order["gother"] = head_of(d_attn, mine), head_of(d_attn, 1 - mine)
    send("kv", far, near)
    relay("kv", 0)
    start("a0", order["part_a"], PAIR)
    start("gpair", order["gother"], PAIR)
    order.after("q0", "kv1")
    relay("q", 0)
    order.after("kvother kv0", f"kv{far}")
    order.after("part_b", "a0", "gpair", "q1")
    groups_a = spread("a", [[0]])
    relay("kv", far, near)
    send("kv", *mids[1:])
    start("b0", order["part_b"], PAIR)
    for _ in bits[1:]:
        groups_a = spread("a", groups_a)
    order["grad"] = jnp.concatenate([order["g0"], order["gpair"]], axis=0)

    order.after("q0 qother", f"kv{mids[1]}", f"kv{far ^ 1}")
    order.after(f"kv{mids[1]}", f"kv{near ^ 1}")
    relay("kv", *mids[1:])
    groups_b = spread("b", [[0]])
    send("q", *mids)
    order["kv_even"] = project("kv", even, "a", groups_a)
    order.after("qother", "kv_even")
    send("q", near)
    order.after("b0 b1", *[f"kv{d ^ 1}" for d in mids[1:]])
    for _ in bits[1:]:
        groups_b = spread("b", groups_b)
    last = ("b", groups_b) if per_f > depth else ("a", groups_a)
    order["kv"] = project("kv", odd, *last, order["kv_even"])

    moved = mids + [near]
    start("passed", jnp.concatenate([order[f"q{d}"] for d in moved], axis=0), 1)
    for d in others[:-1]:
        start(f"keys{d}", order["kv"], d, to_later)
    order.after("grad", "kv")
    for d in others[:-1]:
        start(f"grad{d}", order["grad"], d, to_earlier)
    order.after("kv grad", "passed", *[f"grad{d}" for d in others[:-1]])
    start(f"keys{others[-1]}", order["kv"], others[-1], to_later)
    for i, d in enumerate(moved):
        order[f"q{d ^ 1}"] = order["passed"][i * depth : (i + 1) * depth]
    order.after("q0", *[f"grad{d}" for d in others[:-1]])
    order["q_even"] = project("q", even, "a", groups_a)
    order["q"] = project("q", odd, *last, order["q_even"])
    order.after("q", *[f"grad{d}" for d in others[:-1]])
    for d in others[:-1]:
        start(f"query{d}", order["q"], d, to_earlier)
    start("both", jnp.concatenate([order["q"], order["grad"]], axis=1), others[-1])
    order[f"query{others[-1]}"], order[f"grad{others[-1]}"] = order["both"][:, :HD], order["both"][:, HD:]
    kv, q, grad = order["kv"], order["q"], order["grad"]
    kv_pieces = {d: order[f"kv{d}"] for d in range(n_ctx)}
    q_pieces = {d: order[f"q{d}"] for d in range(n_ctx)}
    kvs = [kv] + [order[f"keys{d}"] for d in group[1:]]
    grads = [grad] + [order[f"grad{d}"] for d in group[1:]]
    qs = [q] + [order[f"query{d}"] for d in group[1:]]

    runs = jnp.stack([c ^ d ^ p for d in group for p in (0, PAIR)])
    blocks = runs * run // BLOCK
    here = runs[:2]

    def limits(query_runs, key_runs, query_blocks, key_blocks):
        chosen = jnp.any(
            selected[query_blocks][:, :, None] == key_blocks[None, None, :], axis=1
        )
        ahead = query_runs[:, None] - key_runs[None, :]
        bound = jnp.where(ahead > 0, FAR, jnp.where(ahead == 0, 0, -FAR))
        return jnp.where(chosen, bound, -FAR).astype(jnp.int32)

    query_limits = limits(here, runs, blocks[:2], blocks)
    key_limits = limits(runs, here, blocks, blocks[:2]).T

    stat, column = local_call(
        functools.partial(forward_kernel, sets, run),
        (
            jax.ShapeDtypeStruct((8, 2 * run), F32),
            jax.ShapeDtypeStruct((2 * run, HD), F32),
        ),
        2 + sets,
    )(query_limits, q, grad, *kvs)
    moved_stats = {d: to_earlier(stat, distance=d) for d in others}
    stats = [stat] + [moved_stats[d] for d in group[1:]]
    dq = local_call(
        functools.partial(query_kernel, sets, run),
        jax.ShapeDtypeStruct((2 * run, HD), BF16),
        3 + sets,
    )(query_limits, q, grad, column, *kvs)
    close = 2
    dkv = local_call(
        functools.partial(key_kernel, close, run),
        jax.ShapeDtypeStruct((2 * run, 2 * HD), F32),
        1 + 3 * close,
        [pltpu.VMEM((2 * run, 2 * HD), F32)],
    )(key_limits[:, : 2 * close], kv, *qs[:close], *grads[:close], *stats[:close])
    dkv = local_call(
        functools.partial(key_kernel, sets - close, run),
        jax.ShapeDtypeStruct((2 * run, 2 * HD), BF16),
        2 + 3 * (sets - close),
        [pltpu.VMEM((2 * run, 2 * HD), F32)],
    )(key_limits[:, 2 * close :], kv, *qs[close:], *grads[close:], *stats[close:], dkv)

    all_grads = jnp.concatenate([dkv, dq], axis=1)
    if n_f != 4 or n_ctx != 2 * n_f:
        whole_w = jnp.zeros((width, 3 * HD), BF16)
        for d in kv_pieces:
            piece = jnp.concatenate([kv_pieces[d], q_pieces[d]], axis=1)
            whole_w = lax.dynamic_update_slice(whole_w, piece, ((c ^ d) * depth, 0))
        partial_out = dot_nt(all_grads, whole_w).astype(BF16)
        total = partial_out[:run].astype(F32) + over_ctx(partial_out[run:], distance=PAIR).astype(F32)
        return lax.psum_scatter(total.astype(BF16), "fsdp", scatter_dimension=1, tiled=True)

    stacked = jnp.concatenate(
        [
            jnp.concatenate([kv_pieces[d] for d in range(n_ctx)], axis=0),
            jnp.concatenate([q_pieces[d] for d in range(n_ctx)], axis=0),
        ],
        axis=1,
    )

    half = per_f // 2
    by_core = functools.partial(over_f, distance=1)
    by_x = functools.partial(over_f, distance=2)
    by_z = functools.partial(over_ctx, distance=PAIR)

    def term(which, e, start=0, size=per_f):
        at = ((f ^ e) ^ (c // 2)) * per_f + start
        rows = lax.dynamic_slice_in_dim(stacked, at, size, axis=0)
        return dot_nt(all_grads[which * run : (which + 1) * run], rows)

    def chip(which, e, *columns):
        return term(which, e, *columns) + by_core(term(which, e ^ 1, *columns).astype(BF16)).astype(F32)

    corner_x = by_x(chip(1, 2, 0, half).astype(BF16))
    corner_z = by_z(chip(1, 2, half, half).astype(BF16))
    for_x = chip(0, 2)
    from_x_a = by_x(for_x[:, :half].astype(BF16))
    for_z = chip(1, 0)
    from_z_b = by_z(for_z[:, half:].astype(BF16))
    here = chip(0, 0)
    from_z_a = by_z((for_z[:, :half] + corner_x.astype(F32)).astype(BF16))
    from_x_b = by_x((for_x[:, half:] + corner_z.astype(F32)).astype(BF16))

    def finish_kernel(swapped_ref, here_ref, x_a, x_b, z_a, z_b, out_ref):
        for i, (x_ref, z_ref) in enumerate(((x_a, z_a), (x_b, z_b))):
            total = here_ref[:, i * half : (i + 1) * half] + x_ref[...].astype(F32) + z_ref[...].astype(F32)
            at = pl.multiple_of((swapped_ref[0] ^ i) * half, HD)
            out_ref[:, pl.ds(at, half)] = total.astype(BF16)

    return local_call(
        finish_kernel, jax.ShapeDtypeStruct((run, per_f), BF16), 5
    )(parity.reshape(1).astype(jnp.int32), here, from_x_a, from_x_b, from_z_a, from_z_b)


def solution(mesh):
    placed = (P("ctx", None), P("ctx", None, "fsdp"), P(), P("ctx", "fsdp"))
    body = functools.partial(shards, mesh.shape["ctx"], mesh.shape["fsdp"])
    return jax.shard_map(
        body, mesh=mesh, in_specs=placed, out_specs=P("ctx", "fsdp"), check_vma=False
    )
```

```python
import functools

import jax
import jax.numpy as jnp
from jax import lax
from jax.experimental import pallas as pl
from jax.experimental.pallas import tpu as pltpu
from jax.sharding import PartitionSpec as P

HD = 128
BLOCK = 512
FAR = 1 << 20
PAIR = 2
F32 = jnp.float32
BF16 = jnp.bfloat16
VMEM_LIMIT = 20 * 1024 * 1024


def swap(array, axis, size, distance, sender=lambda i: True):
    pairs = [(i, i ^ distance) for i in range(size) if sender(i)]
    return lax.ppermute(array, axis, pairs)


class Order:
    def __init__(self):
        self.held = {}

    def __getitem__(self, name):
        return self.held[name]

    def __setitem__(self, name, array):
        self.held[name] = array

    def after(self, names, *first):
        names = names.split() + list(first)
        tied = lax.optimization_barrier([self.held[n] for n in names])
        self.held.update(zip(names, tied))


def dot_nt(a, b):
    return lax.dot_general(a, b, (((1,), (1,)), ((), ())), preferred_element_type=F32)


def dot_nn(a, b):
    return lax.dot_general(a, b, (((1,), (0,)), ((), ())), preferred_element_type=F32)


def masked_scores(products, gap, limits, run):
    scaled = products * (HD ** -0.5)
    parts = [
        jnp.where(gap <= limit, scaled[:, i * run : (i + 1) * run], -jnp.inf)
        for i, limit in enumerate(limits)
    ]
    return jnp.concatenate(parts, axis=1)


def tile_gap(run, by):
    rows = lax.broadcasted_iota(jnp.int32, (run, run), by)
    return lax.broadcasted_iota(jnp.int32, (run, run), 1 - by) - rows


def query_scores(sets, run, half, limit_ref, q_ref, kv_refs):
    gap = tile_gap(run, 0)
    q = q_ref[half * run : (half + 1) * run]
    return [
        masked_scores(
            dot_nt(q, kv_refs[j][:, :HD]),
            gap,
            [limit_ref[half, 2 * j], limit_ref[half, 2 * j + 1]],
            run,
        )
        for j in range(sets)
    ]


def forward_kernel(sets, run, limit_ref, q_ref, grad_ref, *refs):
    kv_refs, (stat_ref, column_ref) = refs[:sets], refs[sets:]
    lane = lax.broadcasted_iota(jnp.int32, (run, HD), 1)
    for half in range(2):
        rows = pl.ds(half * run, run)
        scores = query_scores(sets, run, half, limit_ref, q_ref, kv_refs)
        highest = functools.reduce(
            jnp.maximum, [jnp.max(s, axis=1, keepdims=True) for s in scores]
        )
        expo = [jnp.exp(s - highest) for s in scores]
        inverse = 1.0 / sum(jnp.sum(e, axis=1, keepdims=True) for e in expo)
        attended = sum(
            dot_nn((e * inverse).astype(BF16), kv_refs[j][:, HD:]) for j, e in enumerate(expo)
        ).astype(BF16)
        delta = jnp.sum(
            grad_ref[rows, :].astype(F32) * attended.astype(F32), axis=1, keepdims=True
        )
        stats = jnp.where(
            lane == 0, highest, jnp.where(lane == 1, inverse, delta)
        )
        column_ref[rows, :] = stats
        stat_ref[:, rows] = jnp.transpose(stats)[:8]


def query_kernel(sets, run, limit_ref, q_ref, grad_ref, column_ref, *refs):
    kv_refs, dq_ref = refs[:sets], refs[sets]
    for half in range(2):
        rows = pl.ds(half * run, run)
        scores = query_scores(sets, run, half, limit_ref, q_ref, kv_refs)
        highest, inverse, delta = (column_ref[rows, i : i + 1] for i in range(3))
        grad = grad_ref[rows, :]
        dq = jnp.zeros((run, HD), F32)
        for j, s in enumerate(scores):
            probs = jnp.exp(s - highest) * inverse
            dprobs = dot_nt(grad, kv_refs[j][:, HD:])
            dscores = (probs * (dprobs - delta)).astype(BF16)
            dq += dot_nn(dscores, kv_refs[j][:, :HD])
        dq_ref[rows, :] = (dq * (HD ** -0.5)).astype(BF16)


def key_kernel(sets, run, limit_ref, kv_ref, *refs):
    q_refs, grad_refs, stat_refs = refs[:sets], refs[sets : 2 * sets], refs[2 * sets : 3 * sets]
    before, (out_ref, total_ref) = refs[3 * sets : -2], refs[-2:]
    gap = -tile_gap(run, 0)
    total_ref[...] = before[0][...] if before else jnp.zeros_like(total_ref)
    for half in range(2):
        rows = pl.ds(half * run, run)
        for j in range(sets):
            limits = [limit_ref[half, 2 * j], limit_ref[half, 2 * j + 1]]

            @pl.when(jnp.maximum(*limits) > -FAR)
            def add(rows=rows, j=j, limits=limits):
                q, grad, stat = q_refs[j][...], grad_refs[j][...], stat_refs[j]
                scores = masked_scores(dot_nt(kv_ref[rows, :HD], q), gap, limits, run)
                probs = jnp.exp(scores - stat[0:1, :]) * stat[1:2, :]
                dprobs = dot_nt(kv_ref[rows, HD:], grad)
                dscores = (probs * (dprobs - stat[2:3, :])).astype(BF16)
                total_ref[rows, :HD] += dot_nn(dscores, q) * (HD ** -0.5)
                total_ref[rows, HD:] += dot_nn(probs.astype(BF16), grad)

    out_ref[...] = total_ref[...].astype(out_ref.dtype)


def project_kernel(groups, n_pieces, place_ref, own_ref, *refs):
    parts, pieces = refs[: len(groups)], refs[len(groups) : len(groups) + n_pieces]
    before, (out_ref, partner_ref) = refs[len(groups) + n_pieces : -2], refs[-2:]
    run = own_ref.shape[0]
    for ids, part_ref in zip(groups, parts):
        for i, e in enumerate(ids):
            partner_ref[e] = part_ref[i * run : (i + 1) * run]
    total = before[0][...] if before else None
    for i, piece_ref in enumerate(pieces):
        depth = piece_ref.shape[0]
        at = pl.multiple_of(place_ref[0, i], HD)
        rows = jnp.concatenate(
            [own_ref[:, pl.ds(at, depth)], partner_ref[place_ref[1, i]]], axis=0
        )
        term = dot_nn(rows, piece_ref[...])
        total = term if total is None else total + term
    out_ref[...] = total.astype(out_ref.dtype)


def local_call(kernel, out_shape, n_vmem, scratch=()):
    return pl.pallas_call(
        kernel,
        out_shape=out_shape,
        in_specs=[pl.BlockSpec(memory_space=pltpu.SMEM)]
        + [pl.BlockSpec(memory_space=pltpu.VMEM)] * n_vmem,
        out_specs=jax.tree.map(lambda _: pl.BlockSpec(memory_space=pltpu.VMEM), out_shape),
        scratch_shapes=scratch,
        compiler_params=pltpu.CompilerParams(vmem_limit_bytes=VMEM_LIMIT),
        cost_estimate=pl.CostEstimate(flops=1, bytes_accessed=1, transcendentals=0),
    )


def shards(n_ctx, n_f, inputs, w_qkv, selected, d_attn):
    run, width = inputs.shape
    depth = w_qkv.shape[0]
    per_f = width // n_f
    c = lax.axis_index("ctx")
    f = lax.axis_index("fsdp")
    mine = (c // PAIR) % 2
    over_ctx = functools.partial(swap, axis="ctx", size=n_ctx)
    over_f = functools.partial(swap, axis="fsdp", size=n_f)
    even = [d for d in range(n_ctx) if d % 2 == 0]
    group = [d for d in range(n_ctx) if not d & PAIR]
    sets = len(group)

    def head_of(array, which):
        return lax.dynamic_slice_in_dim(array, which * HD, HD, axis=array.ndim - 1)

    order = Order()
    near, *mids = even[1:]
    parity = c % 2
    bits = [1 << i for i in reversed(range(n_f.bit_length() - 1))]

    def kv_of(which):
        return jnp.concatenate([head_of(w_qkv[:, 1], which), head_of(w_qkv[:, 2], which)], axis=1)

    def q_of(which):
        return head_of(w_qkv[:, 0], which)

    step = depth if per_f > depth else per_f

    def part(which):
        start = f * per_f + (which * step if per_f > depth else 0)
        return lax.dynamic_slice_in_dim(inputs, start, step, axis=1)

    def start(name, array, distance, across=over_ctx):
        order[name] = across(array, distance=distance)

    def send(kind, *ds):
        for d in ds:
            start(f"{kind}{d}", order[kind + ("other" if d & PAIR else "0")], d)

    def relay(kind, *ds):
        for d in ds:
            start(f"{kind}{d ^ 1}", order[f"{kind}{d}"], 1)

    def spread(kind, groups):
        bit = bits[len(groups) - 1]
        held = [order[f"{kind}{i}"] for i in range(len(groups))]
        start(f"{kind}{len(groups)}", jnp.concatenate(held, axis=0) if held[1:] else held[0], bit, over_f)
        return groups + [[e ^ bit for ids in groups for e in ids]]

    def project(kind, ds, x_kind, groups, before=None):
        pieces = [order[f"{kind}{d}"] for d in ds]
        first = jnp.stack([(c ^ d) * depth for d in ds])
        place = jnp.stack([first, (first // per_f) ^ f]).astype(jnp.int32)
        held = [order[f"{x_kind}{i}"] for i in range(len(groups))]
        out = jax.ShapeDtypeStruct((2 * run, pieces[0].shape[1]), F32 if before is None else BF16)
        earlier = [] if before is None else [before]
        return local_call(
            functools.partial(project_kernel, groups, len(ds)),
            out,
            1 + len(held) + len(ds) + len(earlier),
            [pltpu.VMEM((n_f, run, step), BF16)],
        )(place, inputs, *held, *pieces, *earlier)

    def top(d):
        return 1 << (d.bit_length() - 1)

    def to_later(array, distance):
        ordered = top(distance) > PAIR
        return over_ctx(array, distance=distance, sender=lambda i: not (ordered and i & top(distance)))

    def to_earlier(array, distance):
        ordered = top(distance) > PAIR
        return over_ctx(array, distance=distance, sender=lambda i: not ordered or i & top(distance))

    odd = [d ^ 1 for d in even]
    others = group[:0:-1]
    far = mids[0]
    order["kv0"], order["kvother"] = kv_of(mine), kv_of(1 - mine)
    order["part_a"], order["part_b"] = part(parity), part(1 - parity)
    order["q0"], order["qother"] = q_of(mine), q_of(1 - mine)
    order["g0"], order["gother"] = head_of(d_attn, mine), head_of(d_attn, 1 - mine)
    send("kv", far, near)
    relay("kv", 0)
    start("a0", order["part_a"], PAIR)
    start("gpair", order["gother"], PAIR)
    order.after("q0", "kv1")
    relay("q", 0)
    order.after("kvother kv0", f"kv{far}")
    order.after("part_b", "a0", "gpair", "q1")
    groups_a = spread("a", [[0]])
    relay("kv", far, near)
    send("kv", *mids[1:])
    start("b0", order["part_b"], PAIR)
    for _ in bits[1:]:
        groups_a = spread("a", groups_a)
    order["grad"] = jnp.concatenate([order["g0"], order["gpair"]], axis=0)

    order.after("q0 qother", f"kv{mids[1]}", f"kv{far ^ 1}")
    order.after(f"kv{mids[1]}", f"kv{near ^ 1}")
    relay("kv", *mids[1:])
    groups_b = spread("b", [[0]])
    send("q", *mids)
    order["kv_even"] = project("kv", even, "a", groups_a)
    order.after("qother", "kv_even")
    send("q", near)
    order.after("b0 b1", *[f"kv{d ^ 1}" for d in mids[1:]])
    for _ in bits[1:]:
        groups_b = spread("b", groups_b)
    last = ("b", groups_b) if per_f > depth else ("a", groups_a)
    order["kv"] = project("kv", odd, *last, order["kv_even"])

    moved = mids + [near]
    start("passed", jnp.concatenate([order[f"q{d}"] for d in moved], axis=0), 1)
    for d in others[:-1]:
        start(f"keys{d}", order["kv"], d, to_later)
    order.after("grad", "kv")
    for d in others[:-1]:
        start(f"grad{d}", order["grad"], d, to_earlier)
    order.after("kv grad", "passed", *[f"grad{d}" for d in others[:-1]])
    start(f"keys{others[-1]}", order["kv"], others[-1], to_later)
    for i, d in enumerate(moved):
        order[f"q{d ^ 1}"] = order["passed"][i * depth : (i + 1) * depth]
    order.after("q0", *[f"grad{d}" for d in others[:-1]])
    order["q_even"] = project("q", even, "a", groups_a)
    order["q"] = project("q", odd, *last, order["q_even"])
    order.after("q", *[f"grad{d}" for d in others[:-1]])
    for d in others[:-1]:
        start(f"query{d}", order["q"], d, to_earlier)
    start("both", jnp.concatenate([order["q"], order["grad"]], axis=1), others[-1])
    order[f"query{others[-1]}"], order[f"grad{others[-1]}"] = order["both"][:, :HD], order["both"][:, HD:]
    kv, q, grad = order["kv"], order["q"], order["grad"]
    kv_pieces = {d: order[f"kv{d}"] for d in range(n_ctx)}
    q_pieces = {d: order[f"q{d}"] for d in range(n_ctx)}
    kvs = [kv] + [order[f"keys{d}"] for d in group[1:]]
    grads = [grad] + [order[f"grad{d}"] for d in group[1:]]
    qs = [q] + [order[f"query{d}"] for d in group[1:]]

    runs = jnp.stack([c ^ d ^ p for d in group for p in (0, PAIR)])
    blocks = runs * run // BLOCK
    here = runs[:2]

    def limits(query_runs, key_runs, query_blocks, key_blocks):
        chosen = jnp.any(
            selected[query_blocks][:, :, None] == key_blocks[None, None, :], axis=1
        )
        ahead = query_runs[:, None] - key_runs[None, :]
        bound = jnp.where(ahead > 0, FAR, jnp.where(ahead == 0, 0, -FAR))
        return jnp.where(chosen, bound, -FAR).astype(jnp.int32)

    query_limits = limits(here, runs, blocks[:2], blocks)
    key_limits = limits(runs, here, blocks, blocks[:2]).T

    stat, column = local_call(
        functools.partial(forward_kernel, sets, run),
        (
            jax.ShapeDtypeStruct((8, 2 * run), F32),
            jax.ShapeDtypeStruct((2 * run, HD), F32),
        ),
        2 + sets,
    )(query_limits, q, grad, *kvs)
    moved_stats = {d: to_earlier(stat, distance=d) for d in others[:-1]}
    near_stat, both = lax.optimization_barrier((stat, order["both"]))
    moved_stats[others[-1]] = to_earlier(near_stat, distance=others[-1])
    qs[1], grads[1] = both[:, :HD], both[:, HD:]
    stats = [stat] + [moved_stats[d] for d in group[1:]]
    dq = local_call(
        functools.partial(query_kernel, sets, run),
        jax.ShapeDtypeStruct((2 * run, HD), BF16),
        3 + sets,
    )(query_limits, q, grad, column, *kvs)
    close = 2
    dkv = local_call(
        functools.partial(key_kernel, close, run),
        jax.ShapeDtypeStruct((2 * run, 2 * HD), F32),
        1 + 3 * close,
        [pltpu.VMEM((2 * run, 2 * HD), F32)],
    )(key_limits[:, : 2 * close], kv, *qs[:close], *grads[:close], *stats[:close])
    dkv = local_call(
        functools.partial(key_kernel, sets - close, run),
        jax.ShapeDtypeStruct((2 * run, 2 * HD), BF16),
        2 + 3 * (sets - close),
        [pltpu.VMEM((2 * run, 2 * HD), F32)],
    )(key_limits[:, 2 * close :], kv, *qs[close:], *grads[close:], *stats[close:], dkv)

    all_grads = jnp.concatenate([dkv, dq], axis=1)
    if n_f != 4 or n_ctx != 2 * n_f:
        whole_w = jnp.zeros((width, 3 * HD), BF16)
        for d in kv_pieces:
            piece = jnp.concatenate([kv_pieces[d], q_pieces[d]], axis=1)
            whole_w = lax.dynamic_update_slice(whole_w, piece, ((c ^ d) * depth, 0))
        partial_out = dot_nt(all_grads, whole_w).astype(BF16)
        total = partial_out[:run].astype(F32) + over_ctx(partial_out[run:], distance=PAIR).astype(F32)
        return lax.psum_scatter(total.astype(BF16), "fsdp", scatter_dimension=1, tiled=True)

    stacked = jnp.concatenate(
        [
            jnp.concatenate([kv_pieces[d] for d in range(n_ctx)], axis=0),
            jnp.concatenate([q_pieces[d] for d in range(n_ctx)], axis=0),
        ],
        axis=1,
    )

    half = per_f // 2
    by_core = functools.partial(over_f, distance=1)
    by_x = functools.partial(over_f, distance=2)
    by_z = functools.partial(over_ctx, distance=PAIR)

    def term(which, e, start=0, size=per_f):
        at = ((f ^ e) ^ (c // 2)) * per_f + start
        rows = lax.dynamic_slice_in_dim(stacked, at, size, axis=0)
        return dot_nt(all_grads[which * run : (which + 1) * run], rows)

    def chip(which, e, *columns):
        return term(which, e, *columns) + by_core(term(which, e ^ 1, *columns).astype(BF16)).astype(F32)

    corner_x = by_x(chip(1, 2, 0, half).astype(BF16))
    corner_z = by_z(chip(1, 2, half, half).astype(BF16))
    for_x = chip(0, 2)
    from_x_a = by_x(for_x[:, :half].astype(BF16))
    for_z = chip(1, 0)
    from_z_b = by_z(for_z[:, half:].astype(BF16))
    here = chip(0, 0)
    from_z_a = by_z((for_z[:, :half] + corner_x.astype(F32)).astype(BF16))
    from_x_b = by_x((for_x[:, half:] + corner_z.astype(F32)).astype(BF16))

    def finish_kernel(swapped_ref, here_ref, x_a, x_b, z_a, z_b, out_ref):
        for i, (x_ref, z_ref) in enumerate(((x_a, z_a), (x_b, z_b))):
            total = here_ref[:, i * half : (i + 1) * half] + x_ref[...].astype(F32) + z_ref[...].astype(F32)
            at = pl.multiple_of((swapped_ref[0] ^ i) * half, HD)
            out_ref[:, pl.ds(at, half)] = total.astype(BF16)

    return local_call(
        finish_kernel, jax.ShapeDtypeStruct((run, per_f), BF16), 5
    )(parity.reshape(1).astype(jnp.int32), here, from_x_a, from_x_b, from_z_a, from_z_b)


def solution(mesh):
    placed = (P("ctx", None), P("ctx", None, "fsdp"), P(), P("ctx", "fsdp"))
    body = functools.partial(shards, mesh.shape["ctx"], mesh.shape["fsdp"])
    return jax.shard_map(
        body, mesh=mesh, in_specs=placed, out_specs=P("ctx", "fsdp"), check_vma=False
    )
```

```python
import functools

import jax
import jax.numpy as jnp
from jax import lax
from jax.experimental import pallas as pl
from jax.experimental.pallas import tpu as pltpu
from jax.sharding import PartitionSpec as P

HD = 128
BLOCK = 512
FAR = 1 << 20
PAIR = 2
F32 = jnp.float32
BF16 = jnp.bfloat16
VMEM_LIMIT = 20 * 1024 * 1024


def swap(array, axis, size, distance, sender=lambda i: True):
    pairs = [(i, i ^ distance) for i in range(size) if sender(i)]
    return lax.ppermute(array, axis, pairs)


class Order:
    def __init__(self):
        self.held = {}

    def __getitem__(self, name):
        return self.held[name]

    def __setitem__(self, name, array):
        self.held[name] = array

    def after(self, names, *first):
        names = names.split() + list(first)
        tied = lax.optimization_barrier([self.held[n] for n in names])
        self.held.update(zip(names, tied))


def dot_nt(a, b):
    return lax.dot_general(a, b, (((1,), (1,)), ((), ())), preferred_element_type=F32)


def dot_nn(a, b):
    return lax.dot_general(a, b, (((1,), (0,)), ((), ())), preferred_element_type=F32)


def masked_scores(products, gap, limits, run):
    scaled = products * (HD ** -0.5)
    parts = [
        jnp.where(gap <= limit, scaled[:, i * run : (i + 1) * run], -jnp.inf)
        for i, limit in enumerate(limits)
    ]
    return jnp.concatenate(parts, axis=1)


def tile_gap(run, by):
    rows = lax.broadcasted_iota(jnp.int32, (run, run), by)
    return lax.broadcasted_iota(jnp.int32, (run, run), 1 - by) - rows


def query_scores(sets, run, half, limit_ref, q_ref, kv_refs):
    gap = tile_gap(run, 0)
    q = q_ref[half * run : (half + 1) * run]
    return [
        masked_scores(
            dot_nt(q, kv_refs[j][:, :HD]),
            gap,
            [limit_ref[half, 2 * j], limit_ref[half, 2 * j + 1]],
            run,
        )
        for j in range(sets)
    ]


def forward_kernel(sets, run, limit_ref, q_ref, grad_ref, *refs):
    kv_refs, (stat_ref, column_ref) = refs[:sets], refs[sets:]
    lane = lax.broadcasted_iota(jnp.int32, (run, HD), 1)
    for half in range(2):
        rows = pl.ds(half * run, run)
        scores = query_scores(sets, run, half, limit_ref, q_ref, kv_refs)
        highest = functools.reduce(
            jnp.maximum, [jnp.max(s, axis=1, keepdims=True) for s in scores]
        )
        expo = [jnp.exp(s - highest) for s in scores]
        inverse = 1.0 / sum(jnp.sum(e, axis=1, keepdims=True) for e in expo)
        attended = sum(
            dot_nn((e * inverse).astype(BF16), kv_refs[j][:, HD:]) for j, e in enumerate(expo)
        ).astype(BF16)
        delta = jnp.sum(
            grad_ref[rows, :].astype(F32) * attended.astype(F32), axis=1, keepdims=True
        )
        stats = jnp.where(
            lane == 0, highest, jnp.where(lane == 1, inverse, delta)
        )
        column_ref[rows, :] = stats
        stat_ref[:, rows] = jnp.transpose(stats)[:8]


def query_kernel(sets, run, limit_ref, q_ref, grad_ref, column_ref, *refs):
    kv_refs, dq_ref = refs[:sets], refs[sets]
    for half in range(2):
        rows = pl.ds(half * run, run)
        scores = query_scores(sets, run, half, limit_ref, q_ref, kv_refs)
        highest, inverse, delta = (column_ref[rows, i : i + 1] for i in range(3))
        grad = grad_ref[rows, :]
        dq = jnp.zeros((run, HD), F32)
        for j, s in enumerate(scores):
            probs = jnp.exp(s - highest) * inverse
            dprobs = dot_nt(grad, kv_refs[j][:, HD:])
            dscores = (probs * (dprobs - delta)).astype(BF16)
            dq += dot_nn(dscores, kv_refs[j][:, :HD])
        dq_ref[rows, :] = (dq * (HD ** -0.5)).astype(BF16)


def key_kernel(sets, run, limit_ref, kv_ref, *refs):
    q_refs, grad_refs, stat_refs = refs[:sets], refs[sets : 2 * sets], refs[2 * sets : 3 * sets]
    before, (out_ref, total_ref) = refs[3 * sets : -2], refs[-2:]
    gap = -tile_gap(run, 0)
    total_ref[...] = before[0][...] if before else jnp.zeros_like(total_ref)
    for half in range(2):
        rows = pl.ds(half * run, run)
        for j in range(sets):
            limits = [limit_ref[half, 2 * j], limit_ref[half, 2 * j + 1]]

            @pl.when(jnp.maximum(*limits) > -FAR)
            def add(rows=rows, j=j, limits=limits):
                q, grad, stat = q_refs[j][...], grad_refs[j][...], stat_refs[j]
                scores = masked_scores(dot_nt(kv_ref[rows, :HD], q), gap, limits, run)
                probs = jnp.exp(scores - stat[0:1, :]) * stat[1:2, :]
                dprobs = dot_nt(kv_ref[rows, HD:], grad)
                dscores = (probs * (dprobs - stat[2:3, :])).astype(BF16)
                total_ref[rows, :HD] += dot_nn(dscores, q) * (HD ** -0.5)
                total_ref[rows, HD:] += dot_nn(probs.astype(BF16), grad)

    out_ref[...] = total_ref[...].astype(out_ref.dtype)


def project_kernel(groups, n_pieces, place_ref, own_ref, *refs):
    parts, pieces = refs[: len(groups)], refs[len(groups) : len(groups) + n_pieces]
    before, (out_ref, partner_ref) = refs[len(groups) + n_pieces : -2], refs[-2:]
    run = own_ref.shape[0]
    for ids, part_ref in zip(groups, parts):
        for i, e in enumerate(ids):
            partner_ref[e] = part_ref[i * run : (i + 1) * run]
    total = before[0][...] if before else None
    for i, piece_ref in enumerate(pieces):
        depth = piece_ref.shape[0]
        at = pl.multiple_of(place_ref[0, i], HD)
        rows = jnp.concatenate(
            [own_ref[:, pl.ds(at, depth)], partner_ref[place_ref[1, i]]], axis=0
        )
        term = dot_nn(rows, piece_ref[...])
        total = term if total is None else total + term
    out_ref[...] = total.astype(out_ref.dtype)


def local_call(kernel, out_shape, n_vmem, scratch=()):
    return pl.pallas_call(
        kernel,
        out_shape=out_shape,
        in_specs=[pl.BlockSpec(memory_space=pltpu.SMEM)]
        + [pl.BlockSpec(memory_space=pltpu.VMEM)] * n_vmem,
        out_specs=jax.tree.map(lambda _: pl.BlockSpec(memory_space=pltpu.VMEM), out_shape),
        scratch_shapes=scratch,
        compiler_params=pltpu.CompilerParams(vmem_limit_bytes=VMEM_LIMIT),
        cost_estimate=pl.CostEstimate(flops=1, bytes_accessed=1, transcendentals=0),
    )


def shards(n_ctx, n_f, inputs, w_qkv, selected, d_attn):
    run, width = inputs.shape
    depth = w_qkv.shape[0]
    per_f = width // n_f
    c = lax.axis_index("ctx")
    f = lax.axis_index("fsdp")
    mine = (c // PAIR) % 2
    over_ctx = functools.partial(swap, axis="ctx", size=n_ctx)
    over_f = functools.partial(swap, axis="fsdp", size=n_f)
    even = [d for d in range(n_ctx) if d % 2 == 0]
    group = [d for d in range(n_ctx) if not d & PAIR]
    sets = len(group)

    def head_of(array, which):
        return lax.dynamic_slice_in_dim(array, which * HD, HD, axis=array.ndim - 1)

    order = Order()
    near, *mids = even[1:]
    parity = c % 2
    bits = [1 << i for i in reversed(range(n_f.bit_length() - 1))]

    def kv_of(which):
        return jnp.concatenate([head_of(w_qkv[:, 1], which), head_of(w_qkv[:, 2], which)], axis=1)

    def q_of(which):
        return head_of(w_qkv[:, 0], which)

    step = depth if per_f > depth else per_f

    def part(which):
        start = f * per_f + (which * step if per_f > depth else 0)
        return lax.dynamic_slice_in_dim(inputs, start, step, axis=1)

    def start(name, array, distance, across=over_ctx):
        order[name] = across(array, distance=distance)

    def send(kind, *ds):
        for d in ds:
            start(f"{kind}{d}", order[kind + ("other" if d & PAIR else "0")], d)

    def relay(kind, *ds):
        for d in ds:
            start(f"{kind}{d ^ 1}", order[f"{kind}{d}"], 1)

    def spread(kind, groups):
        bit = bits[len(groups) - 1]
        held = [order[f"{kind}{i}"] for i in range(len(groups))]
        start(f"{kind}{len(groups)}", jnp.concatenate(held, axis=0) if held[1:] else held[0], bit, over_f)
        return groups + [[e ^ bit for ids in groups for e in ids]]

    def project(kind, ds, x_kind, groups, before=None):
        pieces = [order[f"{kind}{d}"] for d in ds]
        first = jnp.stack([(c ^ d) * depth for d in ds])
        place = jnp.stack([first, (first // per_f) ^ f]).astype(jnp.int32)
        held = [order[f"{x_kind}{i}"] for i in range(len(groups))]
        out = jax.ShapeDtypeStruct((2 * run, pieces[0].shape[1]), F32 if before is None else BF16)
        earlier = [] if before is None else [before]
        return local_call(
            functools.partial(project_kernel, groups, len(ds)),
            out,
            1 + len(held) + len(ds) + len(earlier),
            [pltpu.VMEM((n_f, run, step), BF16)],
        )(place, inputs, *held, *pieces, *earlier)

    def top(d):
        return 1 << (d.bit_length() - 1)

    def to_later(array, distance):
        ordered = top(distance) > PAIR
        return over_ctx(array, distance=distance, sender=lambda i: not (ordered and i & top(distance)))

    def to_earlier(array, distance):
        ordered = top(distance) > PAIR
        return over_ctx(array, distance=distance, sender=lambda i: not ordered or i & top(distance))

    odd = [d ^ 1 for d in even]
    others = group[:0:-1]
    far = mids[0]
    order["kv0"], order["kvother"] = kv_of(mine), kv_of(1 - mine)
    order["part_a"], order["part_b"] = part(parity), part(1 - parity)
    order["q0"], order["qother"] = q_of(mine), q_of(1 - mine)
    order["g0"], order["gother"] = head_of(d_attn, mine), head_of(d_attn, 1 - mine)
    send("kv", far, near)
    relay("kv", 0)
    start("a0", order["part_a"], PAIR)
    start("gpair", order["gother"], PAIR)
    order.after("q0", "kv1")
    relay("q", 0)
    order.after("kvother kv0", f"kv{far}")
    order.after("part_b", "a0", "gpair", "q1")
    groups_a = spread("a", [[0]])
    relay("kv", far, near)
    send("kv", *mids[1:])
    start("b0", order["part_b"], PAIR)
    for _ in bits[1:]:
        groups_a = spread("a", groups_a)
    order["grad"] = jnp.concatenate([order["g0"], order["gpair"]], axis=0)

    order.after("q0 qother", f"kv{mids[1]}", f"kv{far ^ 1}")
    relay("kv", *mids[1:])
    groups_b = spread("b", [[0]])
    send("q", *mids)
    order["kv_even"] = project("kv", even, "a", groups_a)
    order.after("qother", "kv_even")
    send("q", near)
    order.after("b0 b1", *[f"kv{d ^ 1}" for d in mids[1:]], f"kv{near ^ 1}")
    for _ in bits[1:]:
        groups_b = spread("b", groups_b)
    last = ("b", groups_b) if per_f > depth else ("a", groups_a)
    order["kv"] = project("kv", odd, *last, order["kv_even"])

    moved = mids + [near]
    start("passed", jnp.concatenate([order[f"q{d}"] for d in moved], axis=0), 1)
    for d in others[:-1]:
        start(f"keys{d}", order["kv"], d, to_later)
    order.after("grad", "kv")
    for d in others[:-1]:
        start(f"grad{d}", order["grad"], d, to_earlier)
    order.after("kv grad", "passed", *[f"grad{d}" for d in others[:-1]])
    start(f"keys{others[-1]}", order["kv"], others[-1], to_later)
    for i, d in enumerate(moved):
        order[f"q{d ^ 1}"] = order["passed"][i * depth : (i + 1) * depth]
    order.after("q0", *[f"grad{d}" for d in others[:-1]])
    order["q_even"] = project("q", even, "a", groups_a)
    order["q"] = project("q", odd, *last, order["q_even"])
    order.after("q", *[f"grad{d}" for d in others[:-1]])
    for d in others[:-1]:
        start(f"query{d}", order["q"], d, to_earlier)
    start("both", jnp.concatenate([order["q"], order["grad"]], axis=1), others[-1])
    order[f"query{others[-1]}"], order[f"grad{others[-1]}"] = order["both"][:, :HD], order["both"][:, HD:]
    kv, q, grad = order["kv"], order["q"], order["grad"]
    kv_pieces = {d: order[f"kv{d}"] for d in range(n_ctx)}
    q_pieces = {d: order[f"q{d}"] for d in range(n_ctx)}
    kvs = [kv] + [order[f"keys{d}"] for d in group[1:]]
    grads = [grad] + [order[f"grad{d}"] for d in group[1:]]
    qs = [q] + [order[f"query{d}"] for d in group[1:]]

    runs = jnp.stack([c ^ d ^ p for d in group for p in (0, PAIR)])
    blocks = runs * run // BLOCK
    here = runs[:2]

    def limits(query_runs, key_runs, query_blocks, key_blocks):
        chosen = jnp.any(
            selected[query_blocks][:, :, None] == key_blocks[None, None, :], axis=1
        )
        ahead = query_runs[:, None] - key_runs[None, :]
        bound = jnp.where(ahead > 0, FAR, jnp.where(ahead == 0, 0, -FAR))
        return jnp.where(chosen, bound, -FAR).astype(jnp.int32)

    query_limits = limits(here, runs, blocks[:2], blocks)
    key_limits = limits(runs, here, blocks, blocks[:2]).T

    stat, column = local_call(
        functools.partial(forward_kernel, sets, run),
        (
            jax.ShapeDtypeStruct((8, 2 * run), F32),
            jax.ShapeDtypeStruct((2 * run, HD), F32),
        ),
        2 + sets,
    )(query_limits, q, grad, *kvs)
    moved_stats = {d: to_earlier(stat, distance=d) for d in others[:-1]}
    near_stat, both = lax.optimization_barrier((stat, order["both"]))
    moved_stats[others[-1]] = to_earlier(near_stat, distance=others[-1])
    qs[1], grads[1] = both[:, :HD], both[:, HD:]
    stats = [stat] + [moved_stats[d] for d in group[1:]]
    dq = local_call(
        functools.partial(query_kernel, sets, run),
        jax.ShapeDtypeStruct((2 * run, HD), BF16),
        3 + sets,
    )(query_limits, q, grad, column, *kvs)
    close = 2
    dkv = local_call(
        functools.partial(key_kernel, close, run),
        jax.ShapeDtypeStruct((2 * run, 2 * HD), F32),
        1 + 3 * close,
        [pltpu.VMEM((2 * run, 2 * HD), F32)],
    )(key_limits[:, : 2 * close], kv, *qs[:close], *grads[:close], *stats[:close])
    dkv = local_call(
        functools.partial(key_kernel, sets - close, run),
        jax.ShapeDtypeStruct((2 * run, 2 * HD), BF16),
        2 + 3 * (sets - close),
        [pltpu.VMEM((2 * run, 2 * HD), F32)],
    )(key_limits[:, 2 * close :], kv, *qs[close:], *grads[close:], *stats[close:], dkv)

    all_grads = jnp.concatenate([dkv, dq], axis=1)
    if n_f != 4 or n_ctx != 2 * n_f:
        whole_w = jnp.zeros((width, 3 * HD), BF16)
        for d in kv_pieces:
            piece = jnp.concatenate([kv_pieces[d], q_pieces[d]], axis=1)
            whole_w = lax.dynamic_update_slice(whole_w, piece, ((c ^ d) * depth, 0))
        partial_out = dot_nt(all_grads, whole_w).astype(BF16)
        total = partial_out[:run].astype(F32) + over_ctx(partial_out[run:], distance=PAIR).astype(F32)
        return lax.psum_scatter(total.astype(BF16), "fsdp", scatter_dimension=1, tiled=True)

    stacked = jnp.concatenate(
        [
            jnp.concatenate([kv_pieces[d] for d in range(n_ctx)], axis=0),
            jnp.concatenate([q_pieces[d] for d in range(n_ctx)], axis=0),
        ],
        axis=1,
    )

    half = per_f // 2
    by_core = functools.partial(over_f, distance=1)
    by_x = functools.partial(over_f, distance=2)
    by_z = functools.partial(over_ctx, distance=PAIR)

    def term(which, e, start=0, size=per_f):
        at = ((f ^ e) ^ (c // 2)) * per_f + start
        rows = lax.dynamic_slice_in_dim(stacked, at, size, axis=0)
        return dot_nt(all_grads[which * run : (which + 1) * run], rows)

    def chip(which, e, *columns):
        return term(which, e, *columns) + by_core(term(which, e ^ 1, *columns).astype(BF16)).astype(F32)

    corner_x = by_x(chip(1, 2, 0, half).astype(BF16))
    corner_z = by_z(chip(1, 2, half, half).astype(BF16))
    for_x = chip(0, 2)
    from_x_a = by_x(for_x[:, :half].astype(BF16))
    for_z = chip(1, 0)
    from_z_b = by_z(for_z[:, half:].astype(BF16))
    here = chip(0, 0)
    from_z_a = by_z((for_z[:, :half] + corner_x.astype(F32)).astype(BF16))
    from_x_b = by_x((for_x[:, half:] + corner_z.astype(F32)).astype(BF16))

    def finish_kernel(swapped_ref, here_ref, x_a, x_b, z_a, z_b, out_ref):
        for i, (x_ref, z_ref) in enumerate(((x_a, z_a), (x_b, z_b))):
            total = here_ref[:, i * half : (i + 1) * half] + x_ref[...].astype(F32) + z_ref[...].astype(F32)
            at = pl.multiple_of((swapped_ref[0] ^ i) * half, HD)
            out_ref[:, pl.ds(at, half)] = total.astype(BF16)

    return local_call(
        finish_kernel, jax.ShapeDtypeStruct((run, per_f), BF16), 5
    )(parity.reshape(1).astype(jnp.int32), here, from_x_a, from_x_b, from_z_a, from_z_b)


def solution(mesh):
    placed = (P("ctx", None), P("ctx", None, "fsdp"), P(), P("ctx", "fsdp"))
    body = functools.partial(shards, mesh.shape["ctx"], mesh.shape["fsdp"])
    return jax.shard_map(
        body, mesh=mesh, in_specs=placed, out_specs=P("ctx", "fsdp"), check_vma=False
    )
```

```python
import functools

import jax
import jax.numpy as jnp
from jax import lax
from jax.experimental import pallas as pl
from jax.experimental.pallas import tpu as pltpu
from jax.sharding import PartitionSpec as P

HD = 128
BLOCK = 512
FAR = 1 << 20
PAIR = 2
F32 = jnp.float32
BF16 = jnp.bfloat16
VMEM_LIMIT = 20 * 1024 * 1024


def swap(array, axis, size, distance, sender=lambda i: True):
    pairs = [(i, i ^ distance) for i in range(size) if sender(i)]
    return lax.ppermute(array, axis, pairs)


class Order:
    def __init__(self):
        self.held = {}

    def __getitem__(self, name):
        return self.held[name]

    def __setitem__(self, name, array):
        self.held[name] = array

    def after(self, names, *first):
        names = names.split() + list(first)
        tied = lax.optimization_barrier([self.held[n] for n in names])
        self.held.update(zip(names, tied))


def dot_nt(a, b):
    return lax.dot_general(a, b, (((1,), (1,)), ((), ())), preferred_element_type=F32)


def dot_nn(a, b):
    return lax.dot_general(a, b, (((1,), (0,)), ((), ())), preferred_element_type=F32)


def masked_scores(products, gap, limits, run):
    scaled = products * (HD ** -0.5)
    parts = [
        jnp.where(gap <= limit, scaled[:, i * run : (i + 1) * run], -jnp.inf)
        for i, limit in enumerate(limits)
    ]
    return jnp.concatenate(parts, axis=1)


def tile_gap(run, by):
    rows = lax.broadcasted_iota(jnp.int32, (run, run), by)
    return lax.broadcasted_iota(jnp.int32, (run, run), 1 - by) - rows


def query_scores(sets, run, half, limit_ref, q_ref, kv_refs):
    gap = tile_gap(run, 0)
    q = q_ref[half * run : (half + 1) * run]
    return [
        masked_scores(
            dot_nt(q, kv_refs[j][:, :HD]),
            gap,
            [limit_ref[half, 2 * j], limit_ref[half, 2 * j + 1]],
            run,
        )
        for j in range(sets)
    ]


def forward_kernel(sets, run, limit_ref, q_ref, grad_ref, *refs):
    kv_refs, (stat_ref, column_ref) = refs[:sets], refs[sets:]
    lane = lax.broadcasted_iota(jnp.int32, (run, HD), 1)
    for half in range(2):
        rows = pl.ds(half * run, run)
        scores = query_scores(sets, run, half, limit_ref, q_ref, kv_refs)
        highest = functools.reduce(
            jnp.maximum, [jnp.max(s, axis=1, keepdims=True) for s in scores]
        )
        expo = [jnp.exp(s - highest) for s in scores]
        inverse = 1.0 / sum(jnp.sum(e, axis=1, keepdims=True) for e in expo)
        attended = sum(
            dot_nn((e * inverse).astype(BF16), kv_refs[j][:, HD:]) for j, e in enumerate(expo)
        ).astype(BF16)
        delta = jnp.sum(
            grad_ref[rows, :].astype(F32) * attended.astype(F32), axis=1, keepdims=True
        )
        stats = jnp.where(
            lane == 0, highest, jnp.where(lane == 1, inverse, delta)
        )
        column_ref[rows, :] = stats
        stat_ref[:, rows] = jnp.transpose(stats)[:8]


def query_kernel(sets, run, limit_ref, q_ref, grad_ref, column_ref, *refs):
    kv_refs, dq_ref = refs[:sets], refs[sets]
    for half in range(2):
        rows = pl.ds(half * run, run)
        scores = query_scores(sets, run, half, limit_ref, q_ref, kv_refs)
        highest, inverse, delta = (column_ref[rows, i : i + 1] for i in range(3))
        grad = grad_ref[rows, :]
        dq = jnp.zeros((run, HD), F32)
        for j, s in enumerate(scores):
            probs = jnp.exp(s - highest) * inverse
            dprobs = dot_nt(grad, kv_refs[j][:, HD:])
            dscores = (probs * (dprobs - delta)).astype(BF16)
            dq += dot_nn(dscores, kv_refs[j][:, :HD])
        dq_ref[rows, :] = (dq * (HD ** -0.5)).astype(BF16)


def key_kernel(sets, run, limit_ref, kv_ref, *refs):
    q_refs, grad_refs, stat_refs = refs[:sets], refs[sets : 2 * sets], refs[2 * sets : 3 * sets]
    before, (out_ref, total_ref) = refs[3 * sets : -2], refs[-2:]
    gap = -tile_gap(run, 0)
    total_ref[...] = before[0][...] if before else jnp.zeros_like(total_ref)
    for half in range(2):
        rows = pl.ds(half * run, run)
        for j in range(sets):
            limits = [limit_ref[half, 2 * j], limit_ref[half, 2 * j + 1]]

            @pl.when(jnp.maximum(*limits) > -FAR)
            def add(rows=rows, j=j, limits=limits):
                q, grad, stat = q_refs[j][...], grad_refs[j][...], stat_refs[j]
                scores = masked_scores(dot_nt(kv_ref[rows, :HD], q), gap, limits, run)
                probs = jnp.exp(scores - stat[0:1, :]) * stat[1:2, :]
                dprobs = dot_nt(kv_ref[rows, HD:], grad)
                dscores = (probs * (dprobs - stat[2:3, :])).astype(BF16)
                total_ref[rows, :HD] += dot_nn(dscores, q) * (HD ** -0.5)
                total_ref[rows, HD:] += dot_nn(probs.astype(BF16), grad)

    out_ref[...] = total_ref[...].astype(out_ref.dtype)


def project_kernel(groups, n_pieces, place_ref, own_ref, *refs):
    parts, pieces = refs[: len(groups)], refs[len(groups) : len(groups) + n_pieces]
    before, (out_ref, partner_ref) = refs[len(groups) + n_pieces : -2], refs[-2:]
    run = own_ref.shape[0]
    for ids, part_ref in zip(groups, parts):
        for i, e in enumerate(ids):
            partner_ref[e] = part_ref[i * run : (i + 1) * run]
    total = before[0][...] if before else None
    for i, piece_ref in enumerate(pieces):
        depth = piece_ref.shape[0]
        at = pl.multiple_of(place_ref[0, i], HD)
        rows = jnp.concatenate(
            [own_ref[:, pl.ds(at, depth)], partner_ref[place_ref[1, i]]], axis=0
        )
        term = dot_nn(rows, piece_ref[...])
        total = term if total is None else total + term
    out_ref[...] = total.astype(out_ref.dtype)


def local_call(kernel, out_shape, n_vmem, scratch=()):
    return pl.pallas_call(
        kernel,
        out_shape=out_shape,
        in_specs=[pl.BlockSpec(memory_space=pltpu.SMEM)]
        + [pl.BlockSpec(memory_space=pltpu.VMEM)] * n_vmem,
        out_specs=jax.tree.map(lambda _: pl.BlockSpec(memory_space=pltpu.VMEM), out_shape),
        scratch_shapes=scratch,
        compiler_params=pltpu.CompilerParams(vmem_limit_bytes=VMEM_LIMIT),
        cost_estimate=pl.CostEstimate(flops=1, bytes_accessed=1, transcendentals=0),
    )


def shards(n_ctx, n_f, inputs, w_qkv, selected, d_attn):
    run, width = inputs.shape
    depth = w_qkv.shape[0]
    per_f = width // n_f
    c = lax.axis_index("ctx")
    f = lax.axis_index("fsdp")
    mine = (c // PAIR) % 2
    over_ctx = functools.partial(swap, axis="ctx", size=n_ctx)
    over_f = functools.partial(swap, axis="fsdp", size=n_f)
    even = [d for d in range(n_ctx) if d % 2 == 0]
    group = [d for d in range(n_ctx) if not d & PAIR]
    sets = len(group)

    def head_of(array, which):
        return lax.dynamic_slice_in_dim(array, which * HD, HD, axis=array.ndim - 1)

    order = Order()
    near, *mids = even[1:]
    parity = c % 2
    bits = [1 << i for i in reversed(range(n_f.bit_length() - 1))]

    def kv_of(which):
        return jnp.concatenate([head_of(w_qkv[:, 1], which), head_of(w_qkv[:, 2], which)], axis=1)

    def q_of(which):
        return head_of(w_qkv[:, 0], which)

    step = depth if per_f > depth else per_f

    def part(which):
        start = f * per_f + (which * step if per_f > depth else 0)
        return lax.dynamic_slice_in_dim(inputs, start, step, axis=1)

    def start(name, array, distance, across=over_ctx):
        order[name] = across(array, distance=distance)

    def send(kind, *ds):
        for d in ds:
            start(f"{kind}{d}", order[kind + ("other" if d & PAIR else "0")], d)

    def relay(kind, *ds):
        for d in ds:
            start(f"{kind}{d ^ 1}", order[f"{kind}{d}"], 1)

    def spread(kind, groups):
        bit = bits[len(groups) - 1]
        held = [order[f"{kind}{i}"] for i in range(len(groups))]
        start(f"{kind}{len(groups)}", jnp.concatenate(held, axis=0) if held[1:] else held[0], bit, over_f)
        return groups + [[e ^ bit for ids in groups for e in ids]]

    def project(kind, ds, x_kind, groups, before=None):
        pieces = [order[f"{kind}{d}"] for d in ds]
        first = jnp.stack([(c ^ d) * depth for d in ds])
        place = jnp.stack([first, (first // per_f) ^ f]).astype(jnp.int32)
        held = [order[f"{x_kind}{i}"] for i in range(len(groups))]
        out = jax.ShapeDtypeStruct((2 * run, pieces[0].shape[1]), F32 if before is None else BF16)
        earlier = [] if before is None else [before]
        return local_call(
            functools.partial(project_kernel, groups, len(ds)),
            out,
            1 + len(held) + len(ds) + len(earlier),
            [pltpu.VMEM((n_f, run, step), BF16)],
        )(place, inputs, *held, *pieces, *earlier)

    def top(d):
        return 1 << (d.bit_length() - 1)

    def to_later(array, distance):
        ordered = top(distance) > PAIR
        return over_ctx(array, distance=distance, sender=lambda i: not (ordered and i & top(distance)))

    def to_earlier(array, distance):
        ordered = top(distance) > PAIR
        return over_ctx(array, distance=distance, sender=lambda i: not ordered or i & top(distance))

    odd = [d ^ 1 for d in even]
    others = group[:0:-1]
    far = mids[0]
    order["kv0"], order["kvother"] = kv_of(mine), kv_of(1 - mine)
    order["part_a"], order["part_b"] = part(parity), part(1 - parity)
    order["q0"], order["qother"] = q_of(mine), q_of(1 - mine)
    order["g0"], order["gother"] = head_of(d_attn, mine), head_of(d_attn, 1 - mine)
    send("kv", far, near)
    relay("kv", 0)
    start("a0", order["part_a"], PAIR)
    start("gpair", order["gother"], PAIR)
    order.after("q0", "kv1")
    relay("q", 0)
    order.after("kvother kv0", f"kv{far}")
    order.after("part_b", "a0", "gpair", "q1")
    groups_a = spread("a", [[0]])
    relay("kv", far, near)
    send("kv", *mids[1:])
    start("b0", order["part_b"], PAIR)
    for _ in bits[1:]:
        groups_a = spread("a", groups_a)
    order["grad"] = jnp.concatenate([order["g0"], order["gpair"]], axis=0)

    order.after("q0 qother", f"kv{mids[1]}", f"kv{far ^ 1}")
    relay("kv", *mids[1:])
    groups_b = spread("b", [[0]])
    send("q", *mids[::-1])
    order["kv_even"] = project("kv", even, "a", groups_a)
    order.after("qother", "kv_even")
    send("q", near)
    order.after("b0 b1", *[f"kv{d ^ 1}" for d in mids[1:]], f"kv{near ^ 1}")
    for _ in bits[1:]:
        groups_b = spread("b", groups_b)
    last = ("b", groups_b) if per_f > depth else ("a", groups_a)
    order["kv"] = project("kv", odd, *last, order["kv_even"])

    moved = mids + [near]
    start("passed", jnp.concatenate([order[f"q{d}"] for d in moved], axis=0), 1)
    for d in others[:-1]:
        start(f"keys{d}", order["kv"], d, to_later)
    order.after("grad", "kv")
    for d in others[:-1]:
        start(f"grad{d}", order["grad"], d, to_earlier)
    order.after("kv grad", "passed", *[f"grad{d}" for d in others[:-1]])
    start(f"keys{others[-1]}", order["kv"], others[-1], to_later)
    for i, d in enumerate(moved):
        order[f"q{d ^ 1}"] = order["passed"][i * depth : (i + 1) * depth]
    order.after("q0", *[f"grad{d}" for d in others[:-1]])
    order["q_even"] = project("q", even, "a", groups_a)
    order["q"] = project("q", odd, *last, order["q_even"])
    for d in others[:-1]:
        start(f"query{d}", order["q"], d, to_earlier)
    start("both", jnp.concatenate([order["q"], order["grad"]], axis=1), others[-1])
    order[f"query{others[-1]}"], order[f"grad{others[-1]}"] = order["both"][:, :HD], order["both"][:, HD:]
    kv, q, grad = order["kv"], order["q"], order["grad"]
    kv_pieces = {d: order[f"kv{d}"] for d in range(n_ctx)}
    q_pieces = {d: order[f"q{d}"] for d in range(n_ctx)}
    kvs = [kv] + [order[f"keys{d}"] for d in group[1:]]
    grads = [grad] + [order[f"grad{d}"] for d in group[1:]]
    qs = [q] + [order[f"query{d}"] for d in group[1:]]

    runs = jnp.stack([c ^ d ^ p for d in group for p in (0, PAIR)])
    blocks = runs * run // BLOCK
    here = runs[:2]

    def limits(query_runs, key_runs, query_blocks, key_blocks):
        chosen = jnp.any(
            selected[query_blocks][:, :, None] == key_blocks[None, None, :], axis=1
        )
        ahead = query_runs[:, None] - key_runs[None, :]
        bound = jnp.where(ahead > 0, FAR, jnp.where(ahead == 0, 0, -FAR))
        return jnp.where(chosen, bound, -FAR).astype(jnp.int32)

    query_limits = limits(here, runs, blocks[:2], blocks)
    key_limits = limits(runs, here, blocks, blocks[:2]).T

    stat, column = local_call(
        functools.partial(forward_kernel, sets, run),
        (
            jax.ShapeDtypeStruct((8, 2 * run), F32),
            jax.ShapeDtypeStruct((2 * run, HD), F32),
        ),
        2 + sets,
    )(query_limits, q, grad, *kvs)
    moved_stats = {d: to_earlier(stat, distance=d) for d in others[:-1]}
    near_stat, both = lax.optimization_barrier((stat, order["both"]))
    moved_stats[others[-1]] = to_earlier(near_stat, distance=others[-1])
    qs[1], grads[1] = both[:, :HD], both[:, HD:]
    stats = [stat] + [moved_stats[d] for d in group[1:]]
    dq = local_call(
        functools.partial(query_kernel, sets, run),
        jax.ShapeDtypeStruct((2 * run, HD), BF16),
        3 + sets,
    )(query_limits, q, grad, column, *kvs)
    close = 2
    dkv = local_call(
        functools.partial(key_kernel, close, run),
        jax.ShapeDtypeStruct((2 * run, 2 * HD), F32),
        1 + 3 * close,
        [pltpu.VMEM((2 * run, 2 * HD), F32)],
    )(key_limits[:, : 2 * close], kv, *qs[:close], *grads[:close], *stats[:close])
    dkv = local_call(
        functools.partial(key_kernel, sets - close, run),
        jax.ShapeDtypeStruct((2 * run, 2 * HD), BF16),
        2 + 3 * (sets - close),
        [pltpu.VMEM((2 * run, 2 * HD), F32)],
    )(key_limits[:, 2 * close :], kv, *qs[close:], *grads[close:], *stats[close:], dkv)

    all_grads = jnp.concatenate([dkv, dq], axis=1)
    if n_f != 4 or n_ctx != 2 * n_f:
        whole_w = jnp.zeros((width, 3 * HD), BF16)
        for d in kv_pieces:
            piece = jnp.concatenate([kv_pieces[d], q_pieces[d]], axis=1)
            whole_w = lax.dynamic_update_slice(whole_w, piece, ((c ^ d) * depth, 0))
        partial_out = dot_nt(all_grads, whole_w).astype(BF16)
        total = partial_out[:run].astype(F32) + over_ctx(partial_out[run:], distance=PAIR).astype(F32)
        return lax.psum_scatter(total.astype(BF16), "fsdp", scatter_dimension=1, tiled=True)

    stacked = jnp.concatenate(
        [
            jnp.concatenate([kv_pieces[d] for d in range(n_ctx)], axis=0),
            jnp.concatenate([q_pieces[d] for d in range(n_ctx)], axis=0),
        ],
        axis=1,
    )

    half = per_f // 2
    by_core = functools.partial(over_f, distance=1)
    by_x = functools.partial(over_f, distance=2)
    by_z = functools.partial(over_ctx, distance=PAIR)

    def term(which, e, start=0, size=per_f):
        at = ((f ^ e) ^ (c // 2)) * per_f + start
        rows = lax.dynamic_slice_in_dim(stacked, at, size, axis=0)
        return dot_nt(all_grads[which * run : (which + 1) * run], rows)

    def chip(which, e, *columns):
        return term(which, e, *columns) + by_core(term(which, e ^ 1, *columns).astype(BF16)).astype(F32)

    corner_x = by_x(chip(1, 2, 0, half).astype(BF16))
    corner_z = by_z(chip(1, 2, half, half).astype(BF16))
    for_x = chip(0, 2)
    from_x_a = by_x(for_x[:, :half].astype(BF16))
    for_z = chip(1, 0)
    from_z_b = by_z(for_z[:, half:].astype(BF16))
    here = chip(0, 0)
    from_z_a = by_z((for_z[:, :half] + corner_x.astype(F32)).astype(BF16))
    from_x_b = by_x((for_x[:, half:] + corner_z.astype(F32)).astype(BF16))

    def finish_kernel(swapped_ref, here_ref, x_a, x_b, z_a, z_b, out_ref):
        for i, (x_ref, z_ref) in enumerate(((x_a, z_a), (x_b, z_b))):
            total = here_ref[:, i * half : (i + 1) * half] + x_ref[...].astype(F32) + z_ref[...].astype(F32)
            at = pl.multiple_of((swapped_ref[0] ^ i) * half, HD)
            out_ref[:, pl.ds(at, half)] = total.astype(BF16)

    return local_call(
        finish_kernel, jax.ShapeDtypeStruct((run, per_f), BF16), 5
    )(parity.reshape(1).astype(jnp.int32), here, from_x_a, from_x_b, from_z_a, from_z_b)


def solution(mesh):
    placed = (P("ctx", None), P("ctx", None, "fsdp"), P(), P("ctx", "fsdp"))
    body = functools.partial(shards, mesh.shape["ctx"], mesh.shape["fsdp"])
    return jax.shard_map(
        body, mesh=mesh, in_specs=placed, out_specs=P("ctx", "fsdp"), check_vma=False
    )
```
